128 devices in a mesh: ctx: 16 (over y_hi, z, core), tp: 8 (over x, y_lo).
Axes of the slice: x: 4, y: 4 (y_hi: 2, y_lo: 2; y = y_hi * 2 + y_lo), z: 4, core: 2. Of those that a mesh axis runs over, the one named last changes fastest.
Arguments:
- tokens: bfloat16 [8192, 8192], P('ctx', 'tp'), may hold values from -6 to 6
- old_map: int32 [16, 16], replicated, may hold values from 0 to 255, as said below
- new_map: int32 [16, 16], replicated, may hold values from 0 to 255, as said below
- w_query: bfloat16 [8192, 4096], P(None, 'tp'), may hold values from -16 to 16
- key_projection_weight: bfloat16 [8192, 1024], P(None, 'tp'), may hold values from -16 to 16
- value_projection_weight: bfloat16 [8192, 1024], P(None, 'tp'), may hold values from -0.0625 to 0.0625
Outputs:
- attended: bfloat16 [8192, 4096], P('ctx', 'tp')
The draws below stay inside these ranges and needn't reach their ends.
Inputs may be any that keep to these rules, and one draw needn't show every extreme that they name: A permutation of the fine blocks: row a lists the fine blocks of device a in the order of its rows; for every pair of devices a and b exactly one fine block of device a in old_map lies in row b of new_map. `new_map`: row b holds the 8 fine blocks of one coarse block c < 16 in increasing order (fine blocks c*16/2 onwards), then those of coarse block 31-c; each coarse block of the 32 stands in one row.
All inputs are finite; a program needn't handle non-finite values.
Results may differ from the reference program's by a relative error of at most 0.008.
The reference program's roundings to bfloat16 on the way count: a program that leaves them out, or rounds other values in their place, can miss the bound.
Values may be sent and summed in bfloat16 or wider, within the bound.
No kernel may reach another device: no remote copies, remote signals or barrier semaphores. Data moves between devices by JAX's collectives and lax.ppermute only.
A program may use at most 128 MiB of HBM per device.

```python
import math
import jax
import jax.numpy as jnp
from jax import lax

MODEL_WIDTH = 8192
KEY_VALUE_HEADS = 8
HEAD_SIZE = 128
QUERY_HEADS = 32
TOK_DEV = 512
SEQUENCE_TOKENS = 8192
N_CTX = 16


def layout_tables(key):
    count = N_CTX
    half = count // 2
    pairs = jax.random.permutation(jax.random.fold_in(key, 11), count).astype(jnp.int32)
    coarse = jnp.stack([pairs, 2 * count - 1 - pairs], axis=1)
    inner = jnp.arange(half, dtype=jnp.int32)
    new_table = (coarse[:, :, None] * half + inner[None, None, :]).reshape(count, count).astype(jnp.int32)
    column_order = jax.random.permutation(jax.random.fold_in(key, 12), count).astype(jnp.int32)
    row_shift = jax.random.randint(jax.random.fold_in(key, 13), (count,), 0, count)
    inverse = jnp.argsort(column_order).astype(jnp.int32)
    devices = jnp.arange(count, dtype=jnp.int32)
    slots = inverse[(devices[:, None] - row_shift[None, :]) % count]
    held = new_table[devices[None, :], slots]
    shuffles = jax.vmap(lambda subkey: jax.random.permutation(subkey, count))(jax.random.split(jax.random.fold_in(key, 14), count))
    old_table = jnp.take_along_axis(held, shuffles.astype(jnp.int32), axis=1)
    return (old_table.astype(jnp.int32), new_table)


def shared_base(key):
    return jnp.clip(jax.random.normal(key, (MODEL_WIDTH, QUERY_HEADS * HEAD_SIZE), jnp.float32), -4.0, 4.0) / math.sqrt(MODEL_WIDTH)


def draw_old_map(key, part):
    tables = layout_tables(key)
    return tables[0]


def draw_new_map(key, part):
    tables = layout_tables(key)
    return tables[1]


def draw_w_query(key, part):
    base_offset = shared_base(key)
    return base_offset.astype(jnp.bfloat16)


def draw_key_projection_weight(key, part):
    key = jax.random.fold_in(key, 4)
    random_noise = jnp.clip(jax.random.normal(key, (MODEL_WIDTH, KEY_VALUE_HEADS * HEAD_SIZE), jnp.float32), -4.0, 4.0) / math.sqrt(MODEL_WIDTH)
    return random_noise.astype(jnp.bfloat16)


def block_scale(own_key, extent, pieces, least, largest):
    loudness, own = 1.0, jax.random.fold_in(own_key, 6)
    for position, parts in pieces:
        heights = jnp.exp(jax.random.uniform(jax.random.fold_in(own, position), (parts,), jnp.float32, least / len(pieces), largest / len(pieces)))
        loudness = loudness * jnp.repeat(heights, extent[position] // parts).reshape([-1 if axis == position else 1 for axis in range(len(extent))])
    return loudness


def scatter_about(key, shape, deviation, most, cuts=(), kind=jnp.bfloat16):
    values = deviation * jax.random.normal(key, shape, jnp.float32)
    if cuts:
        values = values * block_scale(key, shape, cuts, -0.22, 0.18)
    return jnp.clip(values, -most, most).astype(kind)


def setup_inputs(seed: int = 0) -> dict:
    key_of = jax.random.split(jax.random.key(seed), 7)
    return {
        "tokens": scatter_about(key_of[0], (SEQUENCE_TOKENS, MODEL_WIDTH), 1.0, 6.0, ((0, 16), (1, 8))),
        "old_map": draw_old_map(jax.random.fold_in(key_of[6], 71), 0),
        "new_map": draw_new_map(jax.random.fold_in(key_of[6], 71), 0),
        "w_query": draw_w_query(jax.random.fold_in(key_of[6], 71), 0),
        "key_projection_weight": draw_key_projection_weight(jax.random.fold_in(key_of[6], 71), 0),
        "value_projection_weight": scatter_about(key_of[5], (MODEL_WIDTH, KEY_VALUE_HEADS * HEAD_SIZE), MODEL_WIDTH ** -0.5, 0.0625, ((1, 8),)),
    }


THETA = 500000.0


def layout_positions(table, fine):
    offsets = jnp.arange(fine, dtype=jnp.int32)
    return (table[:, :, None] * fine + offsets[None, None, :]).reshape(-1).astype(jnp.int32)


def apply_rotation(vectors, positions):
    head_dim = vectors.shape[-1]
    half = head_dim // 2
    freqs = jnp.exp(jnp.arange(half, dtype=jnp.float32) * (-2.0 * math.log(THETA) / head_dim))
    angles = positions.astype(jnp.float32)[:, None] * freqs[None, :]
    cosine = jnp.cos(angles)[:, None, :]
    sine = jnp.sin(angles)[:, None, :]
    first = vectors[..., :half]
    second = vectors[..., half:]
    return jnp.concatenate([first * cosine - second * sine, second * cosine + first * sine], axis=-1)


def reference(tokens, old_map, new_map, w_query, key_projection_weight, value_projection_weight):
    fine = TOK_DEV // N_CTX
    old_pos = layout_positions(old_map, fine)
    new_pos = layout_positions(new_map, fine)
    ordered_rows = jnp.zeros_like(tokens).at[old_pos].set(tokens)
    sequence_position = jnp.arange(SEQUENCE_TOKENS, dtype=jnp.int32)
    query_group = QUERY_HEADS // KEY_VALUE_HEADS
    query_matrix = jnp.dot(ordered_rows, w_query, preferred_element_type=jnp.float32).reshape(SEQUENCE_TOKENS, QUERY_HEADS, HEAD_SIZE)
    key = jnp.dot(ordered_rows, key_projection_weight, preferred_element_type=jnp.float32).reshape(SEQUENCE_TOKENS, KEY_VALUE_HEADS, HEAD_SIZE)
    value_matrix = jnp.dot(ordered_rows, value_projection_weight, preferred_element_type=jnp.float32).astype(jnp.bfloat16)
    query_matrix = apply_rotation(query_matrix, sequence_position).astype(jnp.bfloat16).reshape(SEQUENCE_TOKENS, KEY_VALUE_HEADS, query_group, HEAD_SIZE)
    key = apply_rotation(key, sequence_position).astype(jnp.bfloat16)
    value_matrix = value_matrix.reshape(SEQUENCE_TOKENS, KEY_VALUE_HEADS, HEAD_SIZE)
    scale = HEAD_SIZE ** -0.5
    blocks = SEQUENCE_TOKENS // TOK_DEV

    def attend_head(operands):
        head_query, head_key, head_value = operands
        key_f = head_key.astype(jnp.float32)
        value_f = head_value.astype(jnp.float32)

        def attend_block(index):
            begin = index * TOK_DEV
            block = lax.dynamic_slice_in_dim(head_query, begin, TOK_DEV, 0).astype(jnp.float32)
            scores = jnp.einsum('rgd,sd->grs', block, key_f) * scale
            rows = begin + jnp.arange(TOK_DEV, dtype=jnp.int32)
            visible = sequence_position[None, None, :] <= rows[None, :, None]
            top = jnp.max(jnp.where(visible, scores, -1e30), axis=-1, keepdims=True)
            weights = jnp.where(visible, jnp.exp(scores - top), 0.0)
            total = jnp.sum(weights, axis=-1)
            rounded = lax.optimization_barrier(weights.astype(jnp.bfloat16)).astype(jnp.float32)
            mixed = jnp.einsum('grs,sd->grd', rounded, value_f)
            return jnp.transpose(mixed / total[..., None], (1, 0, 2))

        return lax.map(attend_block, jnp.arange(blocks, dtype=jnp.int32)).reshape(SEQUENCE_TOKENS, query_group, HEAD_SIZE)

    outputs = lax.map(attend_head, (jnp.transpose(query_matrix, (1, 0, 2, 3)), jnp.transpose(key, (1, 0, 2)), jnp.transpose(value_matrix, (1, 0, 2))))
    result = jnp.transpose(outputs, (1, 0, 2, 3)).reshape(SEQUENCE_TOKENS, QUERY_HEADS * HEAD_SIZE)
    return jnp.take(result, new_pos, axis=0).astype(jnp.bfloat16)
```

```python
import functools
import math

import jax
import jax.numpy as jnp
from jax import lax
from jax.experimental import pallas as pl
from jax.experimental.pallas import tpu as pltpu
from jax.sharding import PartitionSpec as P

HEAD = 128
THETA = 500000.0
SCALE = HEAD ** -0.5
FINE = 32
CHUNKS = 2
W = FINE // CHUNKS
ROWS = 16 * W
PAYLOAD = 20 * W
KB = 512
VMEM = pl.BlockSpec(memory_space=pltpu.VMEM)
SMEM = pl.BlockSpec(memory_space=pltpu.SMEM)

CHIPS = [(dh, dz) for dh in range(2) for dz in range(4)]


def shift_x(block, step):
    perm = [(i * 2 + j, ((i + step) % 4) * 2 + j) for i in range(4) for j in range(2)]
    return lax.ppermute(block, "tp", perm)


def swap_y(block):
    return lax.ppermute(block, "tp", [(i, i ^ 1) for i in range(8)])


def shift_ctx(block, dh, dz):
    perm = [
        (h * 8 + z * 2 + c, (h ^ dh) * 8 + ((z + dz) % 4) * 2 + c)
        for h in range(2)
        for z in range(4)
        for c in range(2)
    ]
    return lax.ppermute(block, "ctx", perm)


def swap_core(block):
    return lax.ppermute(block, "ctx", [(i, i ^ 1) for i in range(16)])


def dot(a, b):
    return lax.dot_general(a, b, (((1,), (0,)), ((), ())), preferred_element_type=jnp.float32)


def dot_t(a, b):
    return lax.dot_general(a, b, (((1,), (1,)), ((), ())), preferred_element_type=jnp.float32)


def project_kernel(groups, has_acc, last, *refs):
    features, refs = refs[0], refs[1:]
    blocks, at = [], 0
    for n in groups:
        blocks.append(refs[at : at + n])
        at += n
    wq, wk, wv = refs[at : at + 3]
    at += 3
    acc_in = None
    if has_acc:
        acc_in = refs[at]
        at += 1
    if last:
        info, cosine, sine = refs[at : at + 3]
        at += 3
        outs = refs[at : at + 8]
        acc, heads = refs[at + 8 : at + 10]
    else:
        out, acc = refs[at : at + 2]
    step = pl.program_id(0)

    for i, parts in enumerate(blocks):

        @pl.when(step == i)
        def add(i=i, parts=parts):
            block = parts[0][...] if len(parts) == 1 else jnp.concatenate([p[...] for p in parts], axis=0)
            for lo, hi, w in ((0, 512, wq), (512, 640, wk), (640, 768, wv)):
                value = dot(block, w[...])
                if i > 0:
                    value = value + acc[:, lo:hi]
                elif has_acc:
                    value = value + acc_in[:, lo:hi]
                acc[:, lo:hi] = value

    @pl.when(step == len(blocks) - 1)
    def finish():
        if not last:
            out[...] = acc[...]
            return
        cos, sin = cosine[...], sine[...]

        def rotated(lo):
            vector = acc[:, lo : lo + HEAD]
            return (vector * cos + pltpu.roll(vector, HEAD // 2, 1) * sin).astype(jnp.bfloat16)

        for h in range(4):
            heads[:, h * HEAD : (h + 1) * HEAD] = rotated(h * HEAD)
        key = rotated(512)
        value = acc[:, 640:768].astype(jnp.bfloat16)
        me = info[0]
        high, z = me // 8, lax.rem(me // 2, 4)
        for r, (dh, dz) in enumerate(CHIPS):
            outs[r][0:ROWS, 0:HEAD] = key
            outs[r][0:ROWS, HEAD : 2 * HEAD] = value
            chip = lax.rem(high + dh, 2) * 8 + lax.rem(z + dz, 4) * 2
            for core in range(2):
                k = info[1 + chip + core]
                rows = pl.ds(pl.multiple_of(k * W, W), W)
                for half in range(2):
                    at = ROWS + (core * 2 + half) * W
                    outs[r][at : at + W, :] = heads[rows, half * 256 : half * 256 + 256]


def project(features, blocks, weights, acc=None, tables=None):
    groups = [len(b) for b in blocks]
    flat = [p for b in blocks for p in b]
    whole = lambda shape: pl.BlockSpec(shape, lambda i, f: (0,) * len(shape))
    last = tables is not None
    specs = [whole(p.shape) for p in flat]
    specs += [pl.BlockSpec((1024, w.shape[1]), lambda i, f: (f[i], 0)) for w in weights]
    operands = flat + list(weights)
    if acc is not None:
        specs.append(whole(acc.shape))
        operands.append(acc)
    scratch = [pltpu.VMEM((ROWS, 768), jnp.float32)]
    if last:
        specs += [SMEM, whole((ROWS, HEAD)), whole((ROWS, HEAD))]
        operands += list(tables)
        out_shape = [jax.ShapeDtypeStruct((PAYLOAD, 256), jnp.bfloat16)] * 8
        out_specs = [whole((PAYLOAD, 256))] * 8
        scratch.append(pltpu.VMEM((ROWS, 512), jnp.bfloat16))
    else:
        out_shape = jax.ShapeDtypeStruct((ROWS, 768), jnp.float32)
        out_specs = whole((ROWS, 768))
    return pl.pallas_call(
        functools.partial(project_kernel, groups, acc is not None, last),
        grid_spec=pltpu.PrefetchScalarGridSpec(
            num_scalar_prefetch=1,
            grid=(len(blocks),),
            in_specs=specs,
            out_specs=out_specs,
            scratch_shapes=scratch,
        ),
        out_shape=out_shape,
        compiler_params=pltpu.CompilerParams(vmem_limit_bytes=48 * 2**20),
        name="project",
    )(features, *operands)


def attend_kernel(info, old_map, *refs):
    own = refs[: 8 * CHUNKS]
    other = refs[8 * CHUNKS : 9 * CHUNKS]
    out, query, keys, values, top, total, accum = refs[9 * CHUNKS :]
    me = info[0]
    high, z, core = me // 8, lax.rem(me // 2, 4), lax.rem(me, 2)
    for r, (dh, dz) in enumerate(CHIPS):
        for swapped in range(2):
            source = lax.rem(high + dh, 2) * 8 + lax.rem(z + 4 - dz, 4) * 2 + lax.rem(core + swapped, 2)
            slot = info[3 + source]
            for j in range(CHUNKS):
                ref = other[j].at[r] if swapped else own[j * 8 + r]
                for k in range(16):
                    at = pl.ds(pl.multiple_of(old_map[source * 16 + k] * FINE + j * W, W), W)
                    keys[at, :] = ref[k * W : (k + 1) * W, 0:HEAD]
                    values[at, :] = ref[k * W : (k + 1) * W, HEAD : 2 * HEAD]
                for h in range(4):
                    at = pl.ds(pl.multiple_of(ROWS + (core * 2 + h // 2) * W, W), W)
                    to = (slot // 8) * 1024 + h * 256 + lax.rem(slot, 8) * FINE + j * W
                    query[pl.ds(pl.multiple_of(to, W), W), :] = ref[at, (h % 2) * HEAD : (h % 2 + 1) * HEAD]

    for u in range(2):
        coarse = info[1 + u]
        queries = query[u * 1024 : (u + 1) * 1024, :]
        top[...] = jnp.full(top.shape, -1e30, jnp.float32)
        total[...] = jnp.zeros_like(total)
        accum[...] = jnp.zeros_like(accum)
        whole = (coarse * 256) // KB

        def absorb(block, masked, coarse=coarse, queries=queries):
            start = pl.multiple_of(block * KB, KB)
            scores = dot_t(queries, keys[pl.ds(start, KB), :])
            if masked:
                row = lax.rem(lax.broadcasted_iota(jnp.int32, (1024, KB), 0), 256) + coarse * 256
                visible = lax.broadcasted_iota(jnp.int32, (1024, KB), 1) + start <= row
                scores = jnp.where(visible, scores, -1e30)
            old = top[...]
            new = jnp.maximum(old, jnp.max(scores, axis=-1, keepdims=True))
            factor = jnp.exp((old - new) * SCALE)
            weights = jnp.exp((scores - new[:, :1]) * SCALE)
            if masked:
                weights = jnp.where(visible, weights, 0.0)
            sums = total[...] * factor
            for i in range(KB // HEAD):
                sums = sums + weights[:, i * HEAD : (i + 1) * HEAD]
            total[...] = sums
            accum[...] = accum[...] * factor + dot(
                weights.astype(jnp.bfloat16), values[pl.ds(start, KB), :]
            )
            top[...] = new

        def body(block, carry, absorb=absorb):
            absorb(block, False)
            return carry

        lax.fori_loop(0, whole, body, 0)
        absorb(whole, True)
        result = accum[...] / jnp.sum(total[...], axis=-1, keepdims=True)
        for h in range(4):
            out[u * 256 : (u + 1) * 256, h * HEAD : (h + 1) * HEAD] = result[h * 256 : (h + 1) * 256].astype(
                jnp.bfloat16
            )


def attend(info, old_map, own, other):
    return pl.pallas_call(
        attend_kernel,
        out_shape=jax.ShapeDtypeStruct((512, 512), jnp.bfloat16),
        in_specs=[SMEM, SMEM] + [VMEM] * (9 * CHUNKS),
        out_specs=VMEM,
        scratch_shapes=[
            pltpu.VMEM((2048, HEAD), jnp.bfloat16),
            pltpu.VMEM((8192, HEAD), jnp.bfloat16),
            pltpu.VMEM((8192, HEAD), jnp.bfloat16),
            pltpu.VMEM((1024, HEAD), jnp.float32),
            pltpu.VMEM((1024, HEAD), jnp.float32),
            pltpu.VMEM((1024, HEAD), jnp.float32),
        ],
        compiler_params=pltpu.CompilerParams(vmem_limit_bytes=56 * 2**20),
        name="attend",
    )(info, old_map, *own, *other)


def routing(old_map, new_map, own_index):
    devices = jnp.arange(16, dtype=jnp.int32)
    old_mine = lax.dynamic_index_in_dim(old_map, own_index, 0, keepdims=False)
    new_mine = lax.dynamic_index_in_dim(new_map, own_index, 0, keepdims=False)
    outward = jnp.any(new_map[:, :, None] == old_mine[None, None, :], axis=1)
    send_order = jnp.sum(outward.astype(jnp.int32) * devices[None, :], axis=1)
    inward = jnp.any(old_map[:, :, None] == new_mine[None, None, :], axis=1)
    slot_of = jnp.sum(inward.astype(jnp.int32) * devices[None, :], axis=1)
    coarse = jnp.stack([new_mine[0] // 8, new_mine[8] // 8])
    return (
        jnp.concatenate([own_index[None], send_order]).astype(jnp.int32),
        jnp.concatenate([own_index[None], coarse, slot_of]).astype(jnp.int32),
        old_mine,
    )


def angle_tables(positions):
    half = HEAD // 2
    freqs = jnp.exp(jnp.arange(half, dtype=jnp.float32) * (-2.0 * math.log(THETA) / HEAD))
    angles = positions.astype(jnp.float32)[:, None] * freqs[None, :]
    cosine = jnp.cos(angles)
    sine = jnp.sin(angles)
    return jnp.concatenate([cosine, cosine], axis=1), jnp.concatenate([-sine, sine], axis=1)


def local(tokens, old_map, new_map, w_query, key_projection_weight, value_projection_weight):
    me = lax.axis_index("ctx").astype(jnp.int32)
    place = lax.axis_index("tp").astype(jnp.int32)
    weights = (w_query, key_projection_weight, value_projection_weight)
    send_info, attend_info, old_mine = routing(old_map, new_map, me)
    x, y = place // 2, place % 2
    feature = lambda dx, dy: ((x + dx) % 4) * 2 + (y + dy) % 2
    order = [(0, 0), (3, 0), (1, 0), (0, 1), (3, 1), (2, 0), (1, 1), (2, 1)]
    features = jnp.stack([feature(dx, dy) for dx, dy in order]).astype(jnp.int32)
    chunks = tokens.reshape(16, CHUNKS, W, 1024)
    third = (ROWS // 3) // 16 * 16

    own_side, other_side = [], []
    for j in range(CHUNKS):
        mine = chunks[:, j].reshape(ROWS, 1024)
        left = shift_x(mine, 1)
        right = shift_x(mine, -1)
        across = swap_y(mine)
        left_across = shift_x(across, 1)
        far = shift_x(right, -1)
        right_across = swap_y(right)
        far_across = (
            swap_y(far[:third]),
            shift_x(left_across[third : 2 * third], 1),
            shift_x(right_across[2 * third :], -1),
        )
        positions = old_mine[:, None] * FINE + j * W + jnp.arange(W, dtype=jnp.int32)[None, :]
        cosine, sine = angle_tables(positions.reshape(-1))
        acc = project(features[:4], [(mine,), (left,), (right,), (across,)], weights)
        acc = project(features[4:7], [(left_across,), (far,), (right_across,)], weights, acc)
        sent = project(features[7:], [far_across], weights, acc, (send_info, cosine, sine))
        received = [sent[0]] + [shift_ctx(sent[r], *CHIPS[r]) for r in range(1, 8)]
        own_side += received
        other_side.append(swap_core(jnp.stack(received)))
    return attend(attend_info, old_map.reshape(-1), own_side, other_side)


def solution(mesh):
    return jax.shard_map(
        local,
        mesh=mesh,
        in_specs=(P("ctx", "tp"), P(), P(), P(None, "tp"), P(None, "tp"), P(None, "tp")),
        out_specs=P("ctx", "tp"),
        check_vma=False,
    )
```

```python
import functools
import math

import jax
import jax.numpy as jnp
from jax import lax
from jax.experimental import pallas as pl
from jax.experimental.pallas import tpu as pltpu
from jax.sharding import PartitionSpec as P

HEAD = 128
THETA = 500000.0
SCALE = HEAD ** -0.5
FINE = 32
CHUNKS = 2
W = FINE // CHUNKS
ROWS = 16 * W
PAYLOAD = 20 * W
KB = 512
VMEM = pl.BlockSpec(memory_space=pltpu.VMEM)
SMEM = pl.BlockSpec(memory_space=pltpu.SMEM)

CHIPS = [(dh, dz) for dh in range(2) for dz in range(4)]


def shift_x(block, step):
    perm = [(i * 2 + j, ((i + step) % 4) * 2 + j) for i in range(4) for j in range(2)]
    return lax.ppermute(block, "tp", perm)


def swap_y(block):
    return lax.ppermute(block, "tp", [(i, i ^ 1) for i in range(8)])


def shift_ctx(block, dh, dz):
    perm = [
        (h * 8 + z * 2 + c, (h ^ dh) * 8 + ((z + dz) % 4) * 2 + c)
        for h in range(2)
        for z in range(4)
        for c in range(2)
    ]
    return lax.ppermute(block, "ctx", perm)


def together(*values):
    return lax.optimization_barrier(values)


def after(value, *others):
    return lax.optimization_barrier((value, *others))[0]


def swap_core(block):
    return lax.ppermute(block, "ctx", [(i, i ^ 1) for i in range(16)])


def dot(a, b):
    return lax.dot_general(a, b, (((1,), (0,)), ((), ())), preferred_element_type=jnp.float32)


def dot_t(a, b):
    return lax.dot_general(a, b, (((1,), (1,)), ((), ())), preferred_element_type=jnp.float32)


def project_kernel(groups, has_acc, last, joint, *refs):
    features, refs = refs[0], refs[1:]
    blocks, at = [], 0
    for n in groups:
        blocks.append(refs[at : at + n])
        at += n
    wq, wk, wv = refs[at : at + 3]
    at += 3
    acc_in = None
    if has_acc:
        acc_in = refs[at]
        at += 1
    if last:
        info, cosine, sine = refs[at : at + 3]
        at += 3
        outs = refs[at:-2]
        acc, heads = refs[-2:]
    else:
        out, acc = refs[at : at + 2]
    step = pl.program_id(0)

    for i, parts in enumerate(blocks):

        @pl.when(step == i)
        def add(i=i, parts=parts):
            block = parts[0][...] if len(parts) == 1 else jnp.concatenate([p[...] for p in parts], axis=0)
            for lo, hi, w in ((0, 512, wq), (512, 640, wk), (640, 768, wv)):
                value = dot(block, w[...])
                if i > 0:
                    value = value + acc[:, lo:hi]
                elif has_acc:
                    value = value + acc_in[:, lo:hi]
                acc[:, lo:hi] = value

    @pl.when(step == len(blocks) - 1)
    def finish():
        if not last:
            out[...] = acc[...]
            return
        cos, sin = cosine[...], sine[...]

        def rotated(lo):
            vector = acc[:, lo : lo + HEAD]
            return (vector * cos + pltpu.roll(vector, HEAD // 2, 1) * sin).astype(jnp.bfloat16)

        for h in range(4):
            heads[:, h * HEAD : (h + 1) * HEAD] = rotated(h * HEAD)
        key = rotated(512)
        value = acc[:, 640:768].astype(jnp.bfloat16)
        me = info[0]
        high, z = me // 8, lax.rem(me // 2, 4)
        for payload in outs:
            payload[0:ROWS, 0:HEAD] = key
            payload[0:ROWS, HEAD : 2 * HEAD] = value
        for r, (dh, dz) in enumerate(CHIPS):
            to, base = (outs[4], dz * 4 * W) if joint and dh else (outs[r], 0)
            chip = lax.rem(high + dh, 2) * 8 + lax.rem(z + dz, 4) * 2
            for core in range(2):
                k = info[1 + chip + core]
                rows = pl.ds(pl.multiple_of(k * W, W), W)
                for half in range(2):
                    at = ROWS + base + (core * 2 + half) * W
                    to[at : at + W, :] = heads[rows, half * 256 : half * 256 + 256]


def project(features, blocks, weights, acc=None, tables=None, joint=False):
    groups = [len(b) for b in blocks]
    flat = [p for b in blocks for p in b]
    whole = lambda shape: pl.BlockSpec(shape, lambda i, f: (0,) * len(shape))
    last = tables is not None
    specs = [whole(p.shape) for p in flat]
    specs += [pl.BlockSpec((1024, w.shape[1]), lambda i, f: (f[i], 0)) for w in weights]
    operands = flat + list(weights)
    if acc is not None:
        specs.append(whole(acc.shape))
        operands.append(acc)
    scratch = [pltpu.VMEM((ROWS, 768), jnp.float32)]
    if last:
        specs += [SMEM, whole((ROWS, HEAD)), whole((ROWS, HEAD))]
        operands += list(tables)
        sizes = [PAYLOAD] * 4 + [2 * ROWS] if joint else [PAYLOAD] * 8
        out_shape = [jax.ShapeDtypeStruct((n, 256), jnp.bfloat16) for n in sizes]
        out_specs = [whole((n, 256)) for n in sizes]
        scratch.append(pltpu.VMEM((ROWS, 512), jnp.bfloat16))
    else:
        out_shape = jax.ShapeDtypeStruct((ROWS, 768), jnp.float32)
        out_specs = whole((ROWS, 768))
    return pl.pallas_call(
        functools.partial(project_kernel, groups, acc is not None, last, joint),
        grid_spec=pltpu.PrefetchScalarGridSpec(
            num_scalar_prefetch=1,
            grid=(len(blocks),),
            in_specs=specs,
            out_specs=out_specs,
            scratch_shapes=scratch,
        ),
        out_shape=out_shape,
        compiler_params=pltpu.CompilerParams(vmem_limit_bytes=48 * 2**20),
        name="project",
    )(features, *operands)


def attend_kernel(info, old_map, *refs):
    packed, packed_other, late, late_other = refs[:4], refs[4], refs[5:13], refs[13:15]
    out, query, keys, values, top, total, accum = refs[15:]
    me = info[0]
    high, z, core = me // 8, lax.rem(me // 2, 4), lax.rem(me, 2)
    for r, (dh, dz) in enumerate(CHIPS):
        for swapped in range(2):
            source = lax.rem(high + dh, 2) * 8 + lax.rem(z + 4 - dz, 4) * 2 + lax.rem(core + swapped, 2)
            slot = info[3 + source]
            for j in range(CHUNKS):
                if j == 0:
                    ref, base = (packed_other, (dz * 2 + dh) * PAYLOAD) if swapped else (packed[dz], dh * PAYLOAD)
                else:
                    ref, base = (late_other[r // 4], (r % 4) * PAYLOAD) if swapped else (late[r], 0)
                for k in range(16):
                    at = pl.ds(pl.multiple_of(old_map[source * 16 + k] * FINE + j * W, W), W)
                    rows = slice(base + k * W, base + (k + 1) * W)
                    keys[at, :] = ref[rows, 0:HEAD]
                    values[at, :] = ref[rows, HEAD : 2 * HEAD]
                for h in range(4):
                    at = pl.ds(pl.multiple_of(base + ROWS + (core * 2 + h // 2) * W, W), W)
                    to = (slot // 8) * 1024 + h * 256 + lax.rem(slot, 8) * FINE + j * W
                    query[pl.ds(pl.multiple_of(to, W), W), :] = ref[at, (h % 2) * HEAD : (h % 2 + 1) * HEAD]

    for u in range(2):
        coarse = info[1 + u]
        queries = query[u * 1024 : (u + 1) * 1024, :]
        top[...] = jnp.full(top.shape, -1e30, jnp.float32)
        total[...] = jnp.zeros_like(total)
        accum[...] = jnp.zeros_like(accum)
        whole = (coarse * 256) // KB

        def absorb(block, masked, coarse=coarse, queries=queries):
            start = pl.multiple_of(block * KB, KB)
            scores = dot_t(queries, keys[pl.ds(start, KB), :])
            if masked:
                row = lax.rem(lax.broadcasted_iota(jnp.int32, (1024, KB), 0), 256) + coarse * 256
                visible = lax.broadcasted_iota(jnp.int32, (1024, KB), 1) + start <= row
                scores = jnp.where(visible, scores, -1e30)
            old = top[...]
            new = jnp.maximum(old, jnp.max(scores, axis=-1, keepdims=True))
            factor = jnp.exp((old - new) * SCALE)
            weights = jnp.exp((scores - new[:, :1]) * SCALE)
            if masked:
                weights = jnp.where(visible, weights, 0.0)
            sums = total[...] * factor
            for i in range(KB // HEAD):
                sums = sums + weights[:, i * HEAD : (i + 1) * HEAD]
            total[...] = sums
            accum[...] = accum[...] * factor + dot(
                weights.astype(jnp.bfloat16), values[pl.ds(start, KB), :]
            )
            top[...] = new

        def body(block, carry, absorb=absorb):
            absorb(block, False)
            return carry

        lax.fori_loop(0, whole, body, 0)
        absorb(whole, True)
        result = accum[...] / jnp.sum(total[...], axis=-1, keepdims=True)
        for h in range(4):
            out[u * 256 : (u + 1) * 256, h * HEAD : (h + 1) * HEAD] = result[h * 256 : (h + 1) * 256].astype(
                jnp.bfloat16
            )


def attend(info, old_map, parts):
    return pl.pallas_call(
        attend_kernel,
        out_shape=jax.ShapeDtypeStruct((512, 512), jnp.bfloat16),
        in_specs=[SMEM, SMEM] + [VMEM] * len(parts),
        out_specs=VMEM,
        scratch_shapes=[
            pltpu.VMEM((2048, HEAD), jnp.bfloat16),
            pltpu.VMEM((8192, HEAD), jnp.bfloat16),
            pltpu.VMEM((8192, HEAD), jnp.bfloat16),
            pltpu.VMEM((1024, HEAD), jnp.float32),
            pltpu.VMEM((1024, HEAD), jnp.float32),
            pltpu.VMEM((1024, HEAD), jnp.float32),
        ],
        compiler_params=pltpu.CompilerParams(vmem_limit_bytes=56 * 2**20),
        name="attend",
    )(info, old_map, *parts)


def routing(old_map, new_map, own_index):
    devices = jnp.arange(16, dtype=jnp.int32)
    old_mine = lax.dynamic_index_in_dim(old_map, own_index, 0, keepdims=False)
    new_mine = lax.dynamic_index_in_dim(new_map, own_index, 0, keepdims=False)
    outward = jnp.any(new_map[:, :, None] == old_mine[None, None, :], axis=1)
    send_order = jnp.sum(outward.astype(jnp.int32) * devices[None, :], axis=1)
    inward = jnp.any(old_map[:, :, None] == new_mine[None, None, :], axis=1)
    slot_of = jnp.sum(inward.astype(jnp.int32) * devices[None, :], axis=1)
    coarse = jnp.stack([new_mine[0] // 8, new_mine[8] // 8])
    return (
        jnp.concatenate([own_index[None], send_order]).astype(jnp.int32),
        jnp.concatenate([own_index[None], coarse, slot_of]).astype(jnp.int32),
        old_mine,
    )


def angle_tables(positions):
    half = HEAD // 2
    freqs = jnp.exp(jnp.arange(half, dtype=jnp.float32) * (-2.0 * math.log(THETA) / HEAD))
    angles = positions.astype(jnp.float32)[:, None] * freqs[None, :]
    cosine = jnp.cos(angles)
    sine = jnp.sin(angles)
    return jnp.concatenate([cosine, cosine], axis=1), jnp.concatenate([-sine, sine], axis=1)


def local(tokens, old_map, new_map, w_query, key_projection_weight, value_projection_weight):
    me = lax.axis_index("ctx").astype(jnp.int32)
    place = lax.axis_index("tp").astype(jnp.int32)
    weights = (w_query, key_projection_weight, value_projection_weight)
    send_info, attend_info, old_mine = routing(old_map, new_map, me)
    x, y = place // 2, place % 2
    feature = lambda dx, dy: ((x + dx) % 4) * 2 + (y + dy) % 2
    order = [(0, 0), (3, 0), (1, 0), (0, 1), (3, 1), (2, 0), (1, 1), (2, 1)]
    features = jnp.stack([feature(dx, dy) for dx, dy in order]).astype(jnp.int32)
    chunks = tokens.reshape(16, CHUNKS, W, 1024)
    tables = []
    for j in range(CHUNKS):
        positions = old_mine[:, None] * FINE + j * W + jnp.arange(W, dtype=jnp.int32)[None, :]
        tables.append((send_info, *angle_tables(positions.reshape(-1))))
    early, late = (chunks[:, j].reshape(ROWS, 1024) for j in range(CHUNKS))

    left = shift_x(early, 1)
    right = shift_x(early, -1)
    across = swap_y(early)
    late_across = swap_y(after(late, early))
    left, right, across = together(left, right, across)
    left_across = shift_x(across, 1)
    far = shift_x(right, -1)
    right_across = swap_y(right)
    total = project(features[:4], [(early,), (left,), (right,), (across,)], weights)
    late_across, total = together(late_across, total)
    late = after(late, total)
    late_right = shift_x(late, -1)
    left_across, far = together(left_across, far)
    far_across = shift_x(left_across, 1)
    late_left = shift_x(after(late, left_across), 1)
    total = project(features[4:7], [(left_across,), (far,), (right_across,)], weights, total)
    late_right, far_across, total = together(late_right, far_across, total)
    late_far = shift_x(late_right, -1)
    late_right_across = swap_y(late_right)
    sent = project(features[7:], [(far_across,)], weights, total, tables[0], joint=True)
    partner = shift_ctx(sent[4], 1, 0)
    late_left, late_far, late_right_across, partner = together(late_left, late_far, late_right_across, partner)
    late_left_across = shift_x(late_across, 1)
    late_far_across = shift_x(late_right_across, -1)
    early_parts = [
        jnp.concatenate([sent[dz], partner[:ROWS], partner[ROWS + dz * 4 * W : ROWS + (dz + 1) * 4 * W]], axis=0)
        for dz in range(4)
    ]
    early_parts[1:] = [shift_ctx(early_parts[dz], 0, dz) for dz in range(1, 4)]
    blocks = [(late,), (late_left,), (late_right,), (late_across,)]
    total = project(features[:4], blocks, weights)
    late_far, late_right_across, total = together(late_far, late_right_across, total)
    total = project(features[5:7], [(late_far,), (late_right_across,)], weights, total)
    last = jnp.stack([features[4], features[7]])
    sent = project(last, [(late_left_across,), (late_far_across,)], weights, total, tables[1])
    early_other = swap_core(jnp.concatenate(early_parts, axis=0))
    late_parts = [sent[0]] + [shift_ctx(sent[r], *CHIPS[r]) for r in range(1, 8)]
    late_other = [swap_core(jnp.concatenate(late_parts[at : at + 4], axis=0)) for at in (0, 4)]
    return attend(attend_info, old_map.reshape(-1), [*early_parts, early_other, *late_parts, *late_other])


def solution(mesh):
    return jax.shard_map(
        local,
        mesh=mesh,
        in_specs=(P("ctx", "tp"), P(), P(), P(None, "tp"), P(None, "tp"), P(None, "tp")),
        out_specs=P("ctx", "tp"),
        check_vma=False,
    )
```

```python
import functools
import math

import jax
import jax.numpy as jnp
from jax import lax
from jax.experimental import pallas as pl
from jax.experimental.pallas import tpu as pltpu
from jax.sharding import PartitionSpec as P

HEAD = 128
THETA = 500000.0
SCALE = HEAD ** -0.5
FINE = 32
CHUNKS = 2
W = FINE // CHUNKS
ROWS = 16 * W
PAYLOAD = 20 * W
KB = 512
VMEM = pl.BlockSpec(memory_space=pltpu.VMEM)
SMEM = pl.BlockSpec(memory_space=pltpu.SMEM)

CHIPS = [(dh, dz) for dh in range(2) for dz in range(4)]


def shift_x(block, step):
    perm = [(i * 2 + j, ((i + step) % 4) * 2 + j) for i in range(4) for j in range(2)]
    return lax.ppermute(block, "tp", perm)


def swap_y(block):
    return lax.ppermute(block, "tp", [(i, i ^ 1) for i in range(8)])


def shift_ctx(block, dh, dz):
    perm = [
        (h * 8 + z * 2 + c, (h ^ dh) * 8 + ((z + dz) % 4) * 2 + c)
        for h in range(2)
        for z in range(4)
        for c in range(2)
    ]
    return lax.ppermute(block, "ctx", perm)


def together(*values):
    return lax.optimization_barrier(values)


def after(value, *others):
    return lax.optimization_barrier((value, *others))[0]


def swap_core(block):
    return lax.ppermute(block, "ctx", [(i, i ^ 1) for i in range(16)])


def dot(a, b):
    return lax.dot_general(a, b, (((1,), (0,)), ((), ())), preferred_element_type=jnp.float32)


def dot_t(a, b):
    return lax.dot_general(a, b, (((1,), (1,)), ((), ())), preferred_element_type=jnp.float32)


def project_kernel(groups, has_acc, last, joint, *refs):
    features, refs = refs[0], refs[1:]
    blocks, at = [], 0
    for n in groups:
        blocks.append(refs[at : at + n])
        at += n
    wq, wk, wv = refs[at : at + 3]
    at += 3
    acc_in = None
    if has_acc:
        acc_in = refs[at]
        at += 1
    if last:
        info, cosine, sine = refs[at : at + 3]
        at += 3
        outs = refs[at:-2]
        acc, heads = refs[-2:]
    else:
        out, acc = refs[at : at + 2]
    step = pl.program_id(0)

    for i, parts in enumerate(blocks):

        @pl.when(step == i)
        def add(i=i, parts=parts):
            block = parts[0][...] if len(parts) == 1 else jnp.concatenate([p[...] for p in parts], axis=0)
            for lo, hi, w in ((0, 512, wq), (512, 640, wk), (640, 768, wv)):
                value = dot(block, w[...])
                if i > 0:
                    value = value + acc[:, lo:hi]
                elif has_acc:
                    value = value + acc_in[:, lo:hi]
                acc[:, lo:hi] = value

    @pl.when(step == len(blocks) - 1)
    def finish():
        if not last:
            out[...] = acc[...]
            return
        cos, sin = cosine[...], sine[...]

        def rotated(lo):
            vector = acc[:, lo : lo + HEAD]
            return (vector * cos + pltpu.roll(vector, HEAD // 2, 1) * sin).astype(jnp.bfloat16)

        for h in range(4):
            heads[:, h * HEAD : (h + 1) * HEAD] = rotated(h * HEAD)
        key = rotated(512)
        value = acc[:, 640:768].astype(jnp.bfloat16)
        me = info[0]
        high, z = me // 8, lax.rem(me // 2, 4)
        for payload in outs:
            payload[0:ROWS, 0:HEAD] = key
            payload[0:ROWS, HEAD : 2 * HEAD] = value
        for r, (dh, dz) in enumerate(CHIPS):
            to, base = (outs[4], dz * 4 * W) if joint and dh else (outs[r], 0)
            chip = lax.rem(high + dh, 2) * 8 + lax.rem(z + dz, 4) * 2
            for core in range(2):
                k = info[1 + chip + core]
                rows = pl.ds(pl.multiple_of(k * W, W), W)
                for half in range(2):
                    at = ROWS + base + (core * 2 + half) * W
                    to[at : at + W, :] = heads[rows, half * 256 : half * 256 + 256]


def project(features, blocks, weights, acc=None, tables=None, joint=False):
    groups = [len(b) for b in blocks]
    flat = [p for b in blocks for p in b]
    whole = lambda shape: pl.BlockSpec(shape, lambda i, f: (0,) * len(shape))
    last = tables is not None
    specs = [whole(p.shape) for p in flat]
    specs += [pl.BlockSpec((1024, w.shape[1]), lambda i, f: (f[i], 0)) for w in weights]
    operands = flat + list(weights)
    if acc is not None:
        specs.append(whole(acc.shape))
        operands.append(acc)
    scratch = [pltpu.VMEM((ROWS, 768), jnp.float32)]
    if last:
        specs += [SMEM, whole((ROWS, HEAD)), whole((ROWS, HEAD))]
        operands += list(tables)
        sizes = [PAYLOAD] * 4 + [2 * ROWS] if joint else [PAYLOAD] * 8
        out_shape = [jax.ShapeDtypeStruct((n, 256), jnp.bfloat16) for n in sizes]
        out_specs = [whole((n, 256)) for n in sizes]
        scratch.append(pltpu.VMEM((ROWS, 512), jnp.bfloat16))
    else:
        out_shape = jax.ShapeDtypeStruct((ROWS, 768), jnp.float32)
        out_specs = whole((ROWS, 768))
    return pl.pallas_call(
        functools.partial(project_kernel, groups, acc is not None, last, joint),
        grid_spec=pltpu.PrefetchScalarGridSpec(
            num_scalar_prefetch=1,
            grid=(len(blocks),),
            in_specs=specs,
            out_specs=out_specs,
            scratch_shapes=scratch,
        ),
        out_shape=out_shape,
        compiler_params=pltpu.CompilerParams(vmem_limit_bytes=48 * 2**20),
        name="project",
    )(features, *operands)


def attend_kernel(info, old_map, *refs):
    packed, packed_other, late, late_other = refs[:4], refs[4], refs[5:13], refs[13:15]
    out, query, keys, values, top, total, accum = refs[15:]
    me = info[0]
    high, z, core = me // 8, lax.rem(me // 2, 4), lax.rem(me, 2)
    for r, (dh, dz) in enumerate(CHIPS):
        for swapped in range(2):
            source = lax.rem(high + dh, 2) * 8 + lax.rem(z + 4 - dz, 4) * 2 + lax.rem(core + swapped, 2)
            slot = info[3 + source]
            for j in range(CHUNKS):
                if j == 0:
                    ref, base = (packed_other, (dz * 2 + dh) * PAYLOAD) if swapped else (packed[dz], dh * PAYLOAD)
                else:
                    ref, base = (late_other[r // 4], (r % 4) * PAYLOAD) if swapped else (late[r], 0)
                for k in range(16):
                    at = pl.ds(pl.multiple_of(old_map[source * 16 + k] * FINE + j * W, W), W)
                    rows = slice(base + k * W, base + (k + 1) * W)
                    keys[at, :] = ref[rows, 0:HEAD]
                    values[at, :] = ref[rows, HEAD : 2 * HEAD]
                for h in range(4):
                    at = pl.ds(pl.multiple_of(base + ROWS + (core * 2 + h // 2) * W, W), W)
                    to = (slot // 8) * 1024 + h * 256 + lax.rem(slot, 8) * FINE + j * W
                    query[pl.ds(pl.multiple_of(to, W), W), :] = ref[at, (h % 2) * HEAD : (h % 2 + 1) * HEAD]

    for u in range(2):
        coarse = info[1 + u]
        queries = query[u * 1024 : (u + 1) * 1024, :]
        top[...] = jnp.full(top.shape, -1e30, jnp.float32)
        total[...] = jnp.zeros_like(total)
        accum[...] = jnp.zeros_like(accum)
        whole = (coarse * 256) // KB

        def absorb(block, masked, coarse=coarse, queries=queries):
            start = pl.multiple_of(block * KB, KB)
            scores = dot_t(queries, keys[pl.ds(start, KB), :])
            if masked:
                row = lax.rem(lax.broadcasted_iota(jnp.int32, (1024, KB), 0), 256) + coarse * 256
                visible = lax.broadcasted_iota(jnp.int32, (1024, KB), 1) + start <= row
                scores = jnp.where(visible, scores, -1e30)
            old = top[...]
            new = jnp.maximum(old, jnp.max(scores, axis=-1, keepdims=True))
            factor = jnp.exp((old - new) * SCALE)
            weights = jnp.exp((scores - new[:, :1]) * SCALE)
            if masked:
                weights = jnp.where(visible, weights, 0.0)
            sums = total[...] * factor
            for i in range(KB // HEAD):
                sums = sums + weights[:, i * HEAD : (i + 1) * HEAD]
            total[...] = sums
            accum[...] = accum[...] * factor + dot(
                weights.astype(jnp.bfloat16), values[pl.ds(start, KB), :]
            )
            top[...] = new

        def body(block, carry, absorb=absorb):
            absorb(block, False)
            return carry

        lax.fori_loop(0, whole, body, 0)
        absorb(whole, True)
        result = accum[...] / jnp.sum(total[...], axis=-1, keepdims=True)
        for h in range(4):
            out[u * 256 : (u + 1) * 256, h * HEAD : (h + 1) * HEAD] = result[h * 256 : (h + 1) * 256].astype(
                jnp.bfloat16
            )


def attend(info, old_map, parts):
    return pl.pallas_call(
        attend_kernel,
        out_shape=jax.ShapeDtypeStruct((512, 512), jnp.bfloat16),
        in_specs=[SMEM, SMEM] + [VMEM] * len(parts),
        out_specs=VMEM,
        scratch_shapes=[
            pltpu.VMEM((2048, HEAD), jnp.bfloat16),
            pltpu.VMEM((8192, HEAD), jnp.bfloat16),
            pltpu.VMEM((8192, HEAD), jnp.bfloat16),
            pltpu.VMEM((1024, HEAD), jnp.float32),
            pltpu.VMEM((1024, HEAD), jnp.float32),
            pltpu.VMEM((1024, HEAD), jnp.float32),
        ],
        compiler_params=pltpu.CompilerParams(vmem_limit_bytes=56 * 2**20),
        name="attend",
    )(info, old_map, *parts)


def routing(old_map, new_map, own_index):
    devices = jnp.arange(16, dtype=jnp.int32)
    old_mine = lax.dynamic_index_in_dim(old_map, own_index, 0, keepdims=False)
    new_mine = lax.dynamic_index_in_dim(new_map, own_index, 0, keepdims=False)
    outward = jnp.any(new_map[:, :, None] == old_mine[None, None, :], axis=1)
    send_order = jnp.sum(outward.astype(jnp.int32) * devices[None, :], axis=1)
    inward = jnp.any(old_map[:, :, None] == new_mine[None, None, :], axis=1)
    slot_of = jnp.sum(inward.astype(jnp.int32) * devices[None, :], axis=1)
    coarse = jnp.stack([new_mine[0] // 8, new_mine[8] // 8])
    return (
        jnp.concatenate([own_index[None], send_order]).astype(jnp.int32),
        jnp.concatenate([own_index[None], coarse, slot_of]).astype(jnp.int32),
        old_mine,
    )


def angle_tables(positions):
    half = HEAD // 2
    freqs = jnp.exp(jnp.arange(half, dtype=jnp.float32) * (-2.0 * math.log(THETA) / HEAD))
    angles = positions.astype(jnp.float32)[:, None] * freqs[None, :]
    cosine = jnp.cos(angles)
    sine = jnp.sin(angles)
    return jnp.concatenate([cosine, cosine], axis=1), jnp.concatenate([-sine, sine], axis=1)


def local(tokens, old_map, new_map, w_query, key_projection_weight, value_projection_weight):
    me = lax.axis_index("ctx").astype(jnp.int32)
    place = lax.axis_index("tp").astype(jnp.int32)
    weights = (w_query, key_projection_weight, value_projection_weight)
    send_info, attend_info, old_mine = routing(old_map, new_map, me)
    x, y = place // 2, place % 2
    feature = lambda dx, dy: ((x + dx) % 4) * 2 + (y + dy) % 2
    order = [(0, 0), (3, 0), (1, 0), (0, 1), (3, 1), (2, 0), (1, 1), (2, 1)]
    features = jnp.stack([feature(dx, dy) for dx, dy in order]).astype(jnp.int32)
    chunks = tokens.reshape(16, CHUNKS, W, 1024)
    early, late = (chunks[:, j].reshape(ROWS, 1024) for j in range(CHUNKS))
    tables = []
    for j in range(CHUNKS):
        positions = old_mine[:, None] * FINE + j * W + jnp.arange(W, dtype=jnp.int32)[None, :]
        tables += angle_tables(positions.reshape(-1))
    old_flat = old_map.reshape(-1)

    left = shift_x(early, 1)
    right = shift_x(early, -1)
    across = swap_y(early)
    late_across = swap_y(after(late, early))
    left, right, across, send_info, attend_info, old_flat, *tables = together(
        left, right, across, send_info, attend_info, old_flat, *tables
    )
    left_across = shift_x(across, 1)
    far = shift_x(right, -1)
    right_across = swap_y(right)
    total = project(features[:4], [(early,), (left,), (right,), (across,)], weights)
    late_across, total = together(late_across, total)
    late = after(late, total)
    late_right = shift_x(late, -1)
    left_across, far = together(left_across, far)
    far_across = shift_x(left_across, 1)
    late_left = shift_x(after(late, left_across), 1)
    total = project(features[4:7], [(left_across,), (far,), (right_across,)], weights, total)
    late_right, far_across, total = together(late_right, far_across, total)
    late_far = shift_x(late_right, -1)
    late_right_across = swap_y(late_right)
    sent = project(features[7:], [(far_across,)], weights, total, (send_info, *tables[:2]), joint=True)
    partner = shift_ctx(sent[4], 1, 0)
    late_across, late_left = together(late_across, late_left, sent[0])[:2]
    late_left_across = shift_x(late_across, 1)
    blocks = [(late,), (late_left,), (late_right,), (late_across,)]
    total = project(features[:4], blocks, weights)
    late_far, late_right_across, total = together(late_far, late_right_across, total)
    late_far_across = shift_x(late_right_across, -1)
    partner = after(partner, late_right_across, late_far)
    early_parts = [
        jnp.concatenate([sent[dz], partner[:ROWS], partner[ROWS + dz * 4 * W : ROWS + (dz + 1) * 4 * W]], axis=0)
        for dz in range(4)
    ]
    early_parts = list(together(*early_parts))
    early_parts[1:] = [shift_ctx(early_parts[dz], 0, dz) for dz in range(1, 4)]
    total = project(features[5:7], [(late_far,), (late_right_across,)], weights, total)
    last = jnp.stack([features[4], features[7]])
    tail = [(late_left_across,), (late_far_across,)]
    sent = project(last, tail, weights, total, (send_info, *tables[2:]))
    early_other = swap_core(jnp.concatenate(early_parts, axis=0))
    late_parts = [sent[0]] + [shift_ctx(sent[r], *CHIPS[r]) for r in range(1, 8)]
    late_other = [swap_core(jnp.concatenate(late_parts[at : at + 4], axis=0)) for at in (0, 4)]
    return attend(attend_info, old_flat, [*early_parts, early_other, *late_parts, *late_other])


def solution(mesh):
    return jax.shard_map(
        local,
        mesh=mesh,
        in_specs=(P("ctx", "tp"), P(), P(), P(None, "tp"), P(None, "tp"), P(None, "tp")),
        out_specs=P("ctx", "tp"),
        check_vma=False,
    )
```

```python
import functools
import math

import jax
import jax.numpy as jnp
from jax import lax
from jax.experimental import pallas as pl
from jax.experimental.pallas import tpu as pltpu
from jax.sharding import PartitionSpec as P

HEAD = 128
THETA = 500000.0
SCALE = HEAD ** -0.5
FINE = 32
CHUNKS = 2
W = FINE // CHUNKS
ROWS = 16 * W
PAYLOAD = 20 * W
KB = 512
VMEM = pl.BlockSpec(memory_space=pltpu.VMEM)
SMEM = pl.BlockSpec(memory_space=pltpu.SMEM)

CHIPS = [(dh, dz) for dh in range(2) for dz in range(4)]


def shift_x(block, step):
    perm = [(i * 2 + j, ((i + step) % 4) * 2 + j) for i in range(4) for j in range(2)]
    return lax.ppermute(block, "tp", perm)


def swap_y(block):
    return lax.ppermute(block, "tp", [(i, i ^ 1) for i in range(8)])


def shift_ctx(block, dh, dz):
    perm = [
        (h * 8 + z * 2 + c, (h ^ dh) * 8 + ((z + dz) % 4) * 2 + c)
        for h in range(2)
        for z in range(4)
        for c in range(2)
    ]
    return lax.ppermute(block, "ctx", perm)


def together(*values):
    return lax.optimization_barrier(values)


def after(value, *others):
    return lax.optimization_barrier((value, *others))[0]


def swap_core(block):
    return lax.ppermute(block, "ctx", [(i, i ^ 1) for i in range(16)])


def dot(a, b):
    return lax.dot_general(a, b, (((1,), (0,)), ((), ())), preferred_element_type=jnp.float32)


def dot_t(a, b):
    return lax.dot_general(a, b, (((1,), (1,)), ((), ())), preferred_element_type=jnp.float32)


def project_kernel(groups, has_acc, last, joint, *refs):
    features, refs = refs[0], refs[1:]
    blocks, at = [], 0
    for n in groups:
        blocks.append(refs[at : at + n])
        at += n
    wq, wk, wv = refs[at : at + 3]
    at += 3
    acc_in = None
    if has_acc:
        acc_in = refs[at]
        at += 1
    if last:
        info, cosine, sine = refs[at : at + 3]
        at += 3
        outs = refs[at:-2]
        acc, heads = refs[-2:]
    else:
        out, acc = refs[at : at + 2]
    step = pl.program_id(0)

    for i, parts in enumerate(blocks):

        @pl.when(step == i)
        def add(i=i, parts=parts):
            block = parts[0][...] if len(parts) == 1 else jnp.concatenate([p[...] for p in parts], axis=0)
            for lo, hi, w in ((0, 512, wq[...]), (512, 768, jnp.concatenate([wk[...], wv[...]], axis=1))):
                value = dot(block, w)
                if i > 0:
                    value = value + acc[:, lo:hi]
                elif has_acc:
                    value = value + acc_in[:, lo:hi]
                acc[:, lo:hi] = value

    @pl.when(step == len(blocks) - 1)
    def finish():
        if not last:
            out[...] = acc[...]
            return
        cos, sin = cosine[...], sine[...]

        def rotated(lo):
            vector = acc[:, lo : lo + HEAD]
            return (vector * cos + pltpu.roll(vector, HEAD // 2, 1) * sin).astype(jnp.bfloat16)

        for h in range(4):
            heads[:, h * HEAD : (h + 1) * HEAD] = rotated(h * HEAD)
        key = rotated(512)
        value = acc[:, 640:768].astype(jnp.bfloat16)
        me = info[0]
        high, z = me // 8, lax.rem(me // 2, 4)
        for payload in outs:
            payload[0:ROWS, 0:HEAD] = key
            payload[0:ROWS, HEAD : 2 * HEAD] = value
        for r, (dh, dz) in enumerate(CHIPS):
            to, base = (outs[4], dz * 4 * W) if joint and dh else (outs[r], 0)
            chip = lax.rem(high + dh, 2) * 8 + lax.rem(z + dz, 4) * 2
            for core in range(2):
                k = info[1 + chip + core]
                rows = pl.ds(pl.multiple_of(k * W, W), W)
                for half in range(2):
                    at = ROWS + base + (core * 2 + half) * W
                    to[at : at + W, :] = heads[rows, half * 256 : half * 256 + 256]


def project(features, blocks, weights, acc=None, tables=None, joint=False):
    groups = [len(b) for b in blocks]
    flat = [p for b in blocks for p in b]
    whole = lambda shape: pl.BlockSpec(shape, lambda i, f: (0,) * len(shape))
    last = tables is not None
    specs = [whole(p.shape) for p in flat]
    specs += [pl.BlockSpec((1024, w.shape[1]), lambda i, f: (f[i], 0)) for w in weights]
    operands = flat + list(weights)
    if acc is not None:
        specs.append(whole(acc.shape))
        operands.append(acc)
    scratch = [pltpu.VMEM((ROWS, 768), jnp.float32)]
    if last:
        specs += [SMEM, whole((ROWS, HEAD)), whole((ROWS, HEAD))]
        operands += list(tables)
        sizes = [PAYLOAD] * 4 + [2 * ROWS] if joint else [PAYLOAD] * 8
        out_shape = [jax.ShapeDtypeStruct((n, 256), jnp.bfloat16) for n in sizes]
        out_specs = [whole((n, 256)) for n in sizes]
        scratch.append(pltpu.VMEM((ROWS, 512), jnp.bfloat16))
    else:
        out_shape = jax.ShapeDtypeStruct((ROWS, 768), jnp.float32)
        out_specs = whole((ROWS, 768))
    return pl.pallas_call(
        functools.partial(project_kernel, groups, acc is not None, last, joint),
        grid_spec=pltpu.PrefetchScalarGridSpec(
            num_scalar_prefetch=1,
            grid=(len(blocks),),
            in_specs=specs,
            out_specs=out_specs,
            scratch_shapes=scratch,
        ),
        out_shape=out_shape,
        compiler_params=pltpu.CompilerParams(vmem_limit_bytes=48 * 2**20),
        name="project",
    )(features, *operands)


def attend_kernel(info, old_map, *refs):
    packed, packed_other, late, late_other = refs[:4], refs[4], refs[5:13], refs[13:15]
    out, query, keys, values, top, total, accum = refs[15:]
    me = info[0]
    high, z, core = me // 8, lax.rem(me // 2, 4), lax.rem(me, 2)
    for r, (dh, dz) in enumerate(CHIPS):
        for swapped in range(2):
            source = lax.rem(high + dh, 2) * 8 + lax.rem(z + 4 - dz, 4) * 2 + lax.rem(core + swapped, 2)
            slot = info[3 + source]
            for j in range(CHUNKS):
                if j == 0:
                    ref, base = (packed_other, (dz * 2 + dh) * PAYLOAD) if swapped else (packed[dz], dh * PAYLOAD)
                else:
                    ref, base = (late_other[r // 4], (r % 4) * PAYLOAD) if swapped else (late[r], 0)
                for k in range(16):
                    at = pl.ds(pl.multiple_of(old_map[source * 16 + k] * FINE + j * W, W), W)
                    rows = slice(base + k * W, base + (k + 1) * W)
                    keys[at, :] = ref[rows, 0:HEAD]
                    values[at, :] = ref[rows, HEAD : 2 * HEAD]
                for h in range(4):
                    at = pl.ds(pl.multiple_of(base + ROWS + (core * 2 + h // 2) * W, W), W)
                    to = (slot // 8) * 1024 + h * 256 + lax.rem(slot, 8) * FINE + j * W
                    query[pl.ds(pl.multiple_of(to, W), W), :] = ref[at, (h % 2) * HEAD : (h % 2 + 1) * HEAD]

    for u in range(2):
        coarse = info[1 + u]
        queries = query[u * 1024 : (u + 1) * 1024, :]
        top[...] = jnp.full(top.shape, -1e30, jnp.float32)
        total[...] = jnp.zeros_like(total)
        accum[...] = jnp.zeros_like(accum)
        whole = (coarse * 256) // KB

        def absorb(block, masked, coarse=coarse, queries=queries):
            start = pl.multiple_of(block * KB, KB)
            scores = dot_t(queries, keys[pl.ds(start, KB), :])
            if masked:
                row = lax.rem(lax.broadcasted_iota(jnp.int32, (1024, KB), 0), 256) + coarse * 256
                visible = lax.broadcasted_iota(jnp.int32, (1024, KB), 1) + start <= row
                scores = jnp.where(visible, scores, -1e30)
            old = top[...]
            new = jnp.maximum(old, jnp.max(scores, axis=-1, keepdims=True))
            factor = jnp.exp((old - new) * SCALE)
            weights = jnp.exp((scores - new[:, :1]) * SCALE)
            if masked:
                weights = jnp.where(visible, weights, 0.0)
            sums = total[...] * factor
            for i in range(KB // HEAD):
                sums = sums + weights[:, i * HEAD : (i + 1) * HEAD]
            total[...] = sums
            accum[...] = accum[...] * factor + dot(
                weights.astype(jnp.bfloat16), values[pl.ds(start, KB), :]
            )
            top[...] = new

        def body(block, carry, absorb=absorb):
            absorb(block, False)
            return carry

        lax.fori_loop(0, whole, body, 0)
        absorb(whole, True)
        result = accum[...] / jnp.sum(total[...], axis=-1, keepdims=True)
        for h in range(4):
            out[u * 256 : (u + 1) * 256, h * HEAD : (h + 1) * HEAD] = result[h * 256 : (h + 1) * 256].astype(
                jnp.bfloat16
            )


def attend(info, old_map, parts):
    return pl.pallas_call(
        attend_kernel,
        out_shape=jax.ShapeDtypeStruct((512, 512), jnp.bfloat16),
        in_specs=[SMEM, SMEM] + [VMEM] * len(parts),
        out_specs=VMEM,
        scratch_shapes=[
            pltpu.VMEM((2048, HEAD), jnp.bfloat16),
            pltpu.VMEM((8192, HEAD), jnp.bfloat16),
            pltpu.VMEM((8192, HEAD), jnp.bfloat16),
            pltpu.VMEM((1024, HEAD), jnp.float32),
            pltpu.VMEM((1024, HEAD), jnp.float32),
            pltpu.VMEM((1024, HEAD), jnp.float32),
        ],
        compiler_params=pltpu.CompilerParams(vmem_limit_bytes=56 * 2**20),
        name="attend",
    )(info, old_map, *parts)


def routing(old_map, new_map, own_index):
    devices = jnp.arange(16, dtype=jnp.int32)
    old_mine = lax.dynamic_index_in_dim(old_map, own_index, 0, keepdims=False)
    new_mine = lax.dynamic_index_in_dim(new_map, own_index, 0, keepdims=False)
    outward = jnp.any(new_map[:, :, None] == old_mine[None, None, :], axis=1)
    send_order = jnp.sum(outward.astype(jnp.int32) * devices[None, :], axis=1)
    inward = jnp.any(old_map[:, :, None] == new_mine[None, None, :], axis=1)
    slot_of = jnp.sum(inward.astype(jnp.int32) * devices[None, :], axis=1)
    coarse = jnp.stack([new_mine[0] // 8, new_mine[8] // 8])
    return (
        jnp.concatenate([own_index[None], send_order]).astype(jnp.int32),
        jnp.concatenate([own_index[None], coarse, slot_of]).astype(jnp.int32),
        old_mine,
    )


def angle_tables(positions):
    half = HEAD // 2
    freqs = jnp.exp(jnp.arange(half, dtype=jnp.float32) * (-2.0 * math.log(THETA) / HEAD))
    angles = positions.astype(jnp.float32)[:, None] * freqs[None, :]
    cosine = jnp.cos(angles)
    sine = jnp.sin(angles)
    return jnp.concatenate([cosine, cosine], axis=1), jnp.concatenate([-sine, sine], axis=1)


def local(tokens, old_map, new_map, w_query, key_projection_weight, value_projection_weight):
    me = lax.axis_index("ctx").astype(jnp.int32)
    place = lax.axis_index("tp").astype(jnp.int32)
    weights = (w_query, key_projection_weight, value_projection_weight)
    send_info, attend_info, old_mine = routing(old_map, new_map, me)
    x, y = place // 2, place % 2
    feature = lambda dx, dy: ((x + dx) % 4) * 2 + (y + dy) % 2
    order = [(0, 0), (3, 0), (1, 0), (0, 1), (3, 1), (2, 0), (1, 1), (2, 1)]
    features = jnp.stack([feature(dx, dy) for dx, dy in order]).astype(jnp.int32)
    chunks = tokens.reshape(16, CHUNKS, W, 1024)
    early, late = (chunks[:, j].reshape(ROWS, 1024) for j in range(CHUNKS))
    tables = []
    for j in range(CHUNKS):
        positions = old_mine[:, None] * FINE + j * W + jnp.arange(W, dtype=jnp.int32)[None, :]
        tables += angle_tables(positions.reshape(-1))
    old_flat = old_map.reshape(-1)

    left = shift_x(early, 1)
    right = shift_x(early, -1)
    across = swap_y(early)
    late, left, right, across, send_info, attend_info, old_flat, *tables = together(
        late, left, right, across, send_info, attend_info, old_flat, *tables
    )
    left_across = shift_x(across, 1)
    far = shift_x(right, -1)
    right_across = swap_y(right)
    late_across = swap_y(late)
    total = project(features[:4], [(early,), (left,), (right,), (across,)], weights)
    left_across, far, late = together(left_across, far, after(late, total))
    late_right = shift_x(late, -1)
    far_across = shift_x(left_across, 1)
    right_across = after(right_across, late)
    late_left = shift_x(after(late, right_across), 1)
    total = project(features[4:7], [(left_across,), (far,), (right_across,)], weights, total)
    late_right, late_across = together(late_right, late_across)
    late_far = shift_x(late_right, -1)
    late_right_across = swap_y(late_right)
    far_across = after(far_across, late_right)
    sent = project(features[7:], [(far_across,)], weights, total, (send_info, *tables[:2]), joint=True)
    partner = shift_ctx(sent[4], 1, 0)
    late_across, late_left = together(late_across, late_left, sent[0])[:2]
    late_left_across = shift_x(late_across, 1)
    blocks = [(late,), (late_left,), (late_right,), (late_across,)]
    total = project(features[:4], blocks, weights)
    late_far, late_right_across, total = together(late_far, late_right_across, total)
    late_far_across = shift_x(late_right_across, -1)
    total = project(features[5:7], [(late_far,), (late_right_across,)], weights, total)
    partner, total = together(partner, total)
    early_parts = [
        jnp.concatenate([sent[dz], partner[:ROWS], partner[ROWS + dz * 4 * W : ROWS + (dz + 1) * 4 * W]], axis=0)
        for dz in range(4)
    ]
    early_parts = list(together(*early_parts))
    early_parts[1:] = [shift_ctx(early_parts[dz], 0, dz) for dz in range(1, 4)]
    last = jnp.stack([features[4], features[7]])
    tail = [(late_left_across,), (late_far_across,)]
    sent = project(last, tail, weights, total, (send_info, *tables[2:]))
    early_other = swap_core(jnp.concatenate(early_parts, axis=0))
    late_parts = [sent[0]] + [shift_ctx(sent[r], *CHIPS[r]) for r in range(1, 8)]
    late_other = [swap_core(jnp.concatenate(late_parts[at : at + 4], axis=0)) for at in (0, 4)]
    return attend(attend_info, old_flat, [*early_parts, early_other, *late_parts, *late_other])


def solution(mesh):
    return jax.shard_map(
        local,
        mesh=mesh,
        in_specs=(P("ctx", "tp"), P(), P(), P(None, "tp"), P(None, "tp"), P(None, "tp")),
        out_specs=P("ctx", "tp"),
        check_vma=False,
    )
```

```python
import functools
import math

import jax
import jax.numpy as jnp
from jax import lax
from jax.experimental import pallas as pl
from jax.experimental.pallas import tpu as pltpu
from jax.sharding import PartitionSpec as P

HEAD = 128
THETA = 500000.0
SCALE = HEAD ** -0.5
LOG2E = math.log2(math.e)
FINE = 32
CHUNKS = 2
W = FINE // CHUNKS
ROWS = 16 * W
PAYLOAD = 20 * W
KB = 512
VMEM = pl.BlockSpec(memory_space=pltpu.VMEM)
SMEM = pl.BlockSpec(memory_space=pltpu.SMEM)

CHIPS = [(dh, dz) for dh in range(2) for dz in range(4)]


def shift_x(block, step):
    perm = [(i * 2 + j, ((i + step) % 4) * 2 + j) for i in range(4) for j in range(2)]
    return lax.ppermute(block, "tp", perm)


def swap_y(block):
    return lax.ppermute(block, "tp", [(i, i ^ 1) for i in range(8)])


def shift_ctx(block, dh, dz):
    perm = [
        (h * 8 + z * 2 + c, (h ^ dh) * 8 + ((z + dz) % 4) * 2 + c)
        for h in range(2)
        for z in range(4)
        for c in range(2)
    ]
    return lax.ppermute(block, "ctx", perm)


def together(*values):
    return lax.optimization_barrier(values)


def after(value, *others):
    return lax.optimization_barrier((value, *others))[0]


def swap_core(block):
    return lax.ppermute(block, "ctx", [(i, i ^ 1) for i in range(16)])


def dot(a, b):
    return lax.dot_general(a, b, (((1,), (0,)), ((), ())), preferred_element_type=jnp.float32)


def dot_t(a, b):
    return lax.dot_general(a, b, (((1,), (1,)), ((), ())), preferred_element_type=jnp.float32)


def fold(block, combine):
    result = block[:, :HEAD]
    for at in range(HEAD, block.shape[1], HEAD):
        result = combine(result, block[:, at : at + HEAD])
    return result


def less(block, lanes):
    return jnp.concatenate([block[:, at : at + HEAD] - lanes for at in range(0, block.shape[1], HEAD)], axis=1)


def project_kernel(groups, has_acc, last, joint, *refs):
    features, refs = refs[0], refs[1:]
    blocks, at = [], 0
    for n in groups:
        blocks.append(refs[at : at + n])
        at += n
    wq, wk, wv = refs[at : at + 3]
    at += 3
    acc_in = None
    if has_acc:
        acc_in = refs[at]
        at += 1
    if last:
        info, cosine, sine = refs[at : at + 3]
        at += 3
        outs = refs[at:-2]
        acc, heads = refs[-2:]
    else:
        out, acc = refs[at : at + 2]
    step = pl.program_id(0)

    for i, parts in enumerate(blocks):

        @pl.when(step == i)
        def add(i=i, parts=parts):
            block = parts[0][...] if len(parts) == 1 else jnp.concatenate([p[...] for p in parts], axis=0)
            for lo, hi, w in ((0, 512, wq[...]), (512, 768, jnp.concatenate([wk[...], wv[...]], axis=1))):
                value = dot(block, w)
                if i > 0:
                    value = value + acc[:, lo:hi]
                elif has_acc:
                    value = value + acc_in[:, lo:hi]
                acc[:, lo:hi] = value

    @pl.when(step == len(blocks) - 1)
    def finish():
        if not last:
            out[...] = acc[...]
            return
        cos, sin = cosine[...], sine[...]

        def rotated(lo):
            vector = acc[:, lo : lo + HEAD]
            return (vector * cos + pltpu.roll(vector, HEAD // 2, 1) * sin).astype(jnp.bfloat16)

        for h in range(4):
            heads[:, h * HEAD : (h + 1) * HEAD] = rotated(h * HEAD)
        key = rotated(512)
        value = acc[:, 640:768].astype(jnp.bfloat16)
        me = info[0]
        high, z = me // 8, lax.rem(me // 2, 4)
        for payload in outs:
            payload[0:ROWS, 0:HEAD] = key
            payload[0:ROWS, HEAD : 2 * HEAD] = value
        for r, (dh, dz) in enumerate(CHIPS):
            to, base = (outs[4], dz * 4 * W) if joint and dh else (outs[r], 0)
            chip = lax.rem(high + dh, 2) * 8 + lax.rem(z + dz, 4) * 2
            for core in range(2):
                k = info[1 + chip + core]
                rows = pl.ds(pl.multiple_of(k * W, W), W)
                for half in range(2):
                    at = ROWS + base + (core * 2 + half) * W
                    to[at : at + W, :] = heads[rows, half * 256 : half * 256 + 256]


def project(features, blocks, weights, acc=None, tables=None, joint=False):
    groups = [len(b) for b in blocks]
    flat = [p for b in blocks for p in b]
    whole = lambda shape: pl.BlockSpec(shape, lambda i, f: (0,) * len(shape))
    last = tables is not None
    specs = [whole(p.shape) for p in flat]
    specs += [pl.BlockSpec((1024, w.shape[1]), lambda i, f: (f[i], 0)) for w in weights]
    operands = flat + list(weights)
    if acc is not None:
        specs.append(whole(acc.shape))
        operands.append(acc)
    scratch = [pltpu.VMEM((ROWS, 768), jnp.float32)]
    if last:
        specs += [SMEM, whole((ROWS, HEAD)), whole((ROWS, HEAD))]
        operands += list(tables)
        sizes = [PAYLOAD] * 4 + [2 * ROWS] if joint else [PAYLOAD] * 8
        out_shape = [jax.ShapeDtypeStruct((n, 256), jnp.bfloat16) for n in sizes]
        out_specs = [whole((n, 256)) for n in sizes]
        scratch.append(pltpu.VMEM((ROWS, 512), jnp.bfloat16))
    else:
        out_shape = jax.ShapeDtypeStruct((ROWS, 768), jnp.float32)
        out_specs = whole((ROWS, 768))
    return pl.pallas_call(
        functools.partial(project_kernel, groups, acc is not None, last, joint),
        grid_spec=pltpu.PrefetchScalarGridSpec(
            num_scalar_prefetch=1,
            grid=(len(blocks),),
            in_specs=specs,
            out_specs=out_specs,
            scratch_shapes=scratch,
        ),
        out_shape=out_shape,
        compiler_params=pltpu.CompilerParams(vmem_limit_bytes=48 * 2**20),
        cost_estimate=pl.CostEstimate(flops=1, bytes_accessed=1, transcendentals=0),
        name="project",
    )(features, *operands)


def attend_kernel(info, old_map, *refs):
    packed, packed_other, late, late_other = refs[:4], refs[4], refs[5:13], refs[13:15]
    out, query, keys, values, top, total, accum = refs[15:]
    me = info[0]
    high, z, core = me // 8, lax.rem(me // 2, 4), lax.rem(me, 2)
    for r, (dh, dz) in enumerate(CHIPS):
        for swapped in range(2):
            source = lax.rem(high + dh, 2) * 8 + lax.rem(z + 4 - dz, 4) * 2 + lax.rem(core + swapped, 2)
            slot = info[3 + source]
            for j in range(CHUNKS):
                if j == 0:
                    ref, base = (packed_other, (dz * 2 + dh) * PAYLOAD) if swapped else (packed[dz], dh * PAYLOAD)
                else:
                    ref, base = (late_other[r // 4], (r % 4) * PAYLOAD) if swapped else (late[r], 0)
                for k in range(16):
                    at = pl.ds(pl.multiple_of(old_map[source * 16 + k] * FINE + j * W, W), W)
                    rows = slice(base + k * W, base + (k + 1) * W)
                    keys[at, :] = ref[rows, 0:HEAD]
                    values[at, :] = ref[rows, HEAD : 2 * HEAD]
                for h in range(4):
                    at = pl.ds(pl.multiple_of(base + ROWS + (core * 2 + h // 2) * W, W), W)
                    to = (slot // 8) * 1024 + h * 256 + lax.rem(slot, 8) * FINE + j * W
                    query[pl.ds(pl.multiple_of(to, W), W), :] = ref[at, (h % 2) * HEAD : (h % 2 + 1) * HEAD]

    for u in range(2):
        coarse = info[1 + u]
        queries = query[u * 1024 : (u + 1) * 1024, :]
        top[...] = jnp.full(top.shape, -1e30, jnp.float32)
        total[...] = jnp.zeros_like(total)
        accum[...] = jnp.zeros_like(accum)
        whole = (coarse * 256) // KB

        def absorb(block, masked, coarse=coarse, queries=queries):
            start = pl.multiple_of(block * KB, KB)
            scores = dot_t(queries, keys[pl.ds(start, KB), :])
            if masked:
                row = lax.rem(lax.broadcasted_iota(jnp.int32, (1024, KB), 0), 256) + coarse * 256
                visible = lax.broadcasted_iota(jnp.int32, (1024, KB), 1) + start <= row
                scores = jnp.where(visible, scores, -1e30)
            old = top[...]
            new = jnp.maximum(old, jnp.max(fold(scores, jnp.maximum), axis=-1, keepdims=True))
            factor = jnp.exp2((old - new) * (SCALE * LOG2E))
            weights = jnp.exp2(less(scores, new) * (SCALE * LOG2E))
            if masked:
                weights = jnp.where(visible, weights, 0.0)
            total[...] = total[...] * factor + fold(weights, jnp.add)
            accum[...] = accum[...] * factor + dot(
                weights.astype(jnp.bfloat16), values[pl.ds(start, KB), :]
            )
            top[...] = new

        def body(block, carry, absorb=absorb):
            absorb(block, False)
            return carry

        lax.fori_loop(0, whole, body, 0)
        absorb(whole, True)
        result = accum[...] / jnp.sum(total[...], axis=-1, keepdims=True)
        for h in range(4):
            out[u * 256 : (u + 1) * 256, h * HEAD : (h + 1) * HEAD] = result[h * 256 : (h + 1) * 256].astype(
                jnp.bfloat16
            )


def attend(info, old_map, parts):
    return pl.pallas_call(
        attend_kernel,
        out_shape=jax.ShapeDtypeStruct((512, 512), jnp.bfloat16),
        in_specs=[SMEM, SMEM] + [VMEM] * len(parts),
        out_specs=VMEM,
        scratch_shapes=[
            pltpu.VMEM((2048, HEAD), jnp.bfloat16),
            pltpu.VMEM((8192, HEAD), jnp.bfloat16),
            pltpu.VMEM((8192, HEAD), jnp.bfloat16),
            pltpu.VMEM((1024, HEAD), jnp.float32),
            pltpu.VMEM((1024, HEAD), jnp.float32),
            pltpu.VMEM((1024, HEAD), jnp.float32),
        ],
        compiler_params=pltpu.CompilerParams(vmem_limit_bytes=56 * 2**20),
        name="attend",
    )(info, old_map, *parts)


def routing(old_map, new_map, own_index):
    devices = jnp.arange(16, dtype=jnp.int32)
    old_mine = lax.dynamic_index_in_dim(old_map, own_index, 0, keepdims=False)
    new_mine = lax.dynamic_index_in_dim(new_map, own_index, 0, keepdims=False)
    outward = jnp.any(new_map[:, :, None] == old_mine[None, None, :], axis=1)
    send_order = jnp.sum(outward.astype(jnp.int32) * devices[None, :], axis=1)
    inward = jnp.any(old_map[:, :, None] == new_mine[None, None, :], axis=1)
    slot_of = jnp.sum(inward.astype(jnp.int32) * devices[None, :], axis=1)
    coarse = jnp.stack([new_mine[0] // 8, new_mine[8] // 8])
    return (
        jnp.concatenate([own_index[None], send_order]).astype(jnp.int32),
        jnp.concatenate([own_index[None], coarse, slot_of]).astype(jnp.int32),
        old_mine,
    )


def angle_tables(positions):
    half = HEAD // 2
    freqs = jnp.exp(jnp.arange(half, dtype=jnp.float32) * (-2.0 * math.log(THETA) / HEAD))
    angles = positions.astype(jnp.float32)[:, None] * freqs[None, :]
    cosine = jnp.cos(angles)
    sine = jnp.sin(angles)
    return jnp.concatenate([cosine, cosine], axis=1), jnp.concatenate([-sine, sine], axis=1)


def local(tokens, old_map, new_map, w_query, key_projection_weight, value_projection_weight):
    me = lax.axis_index("ctx").astype(jnp.int32)
    place = lax.axis_index("tp").astype(jnp.int32)
    weights = (w_query, key_projection_weight, value_projection_weight)
    send_info, attend_info, old_mine = routing(old_map, new_map, me)
    x, y = place // 2, place % 2
    feature = lambda dx, dy: ((x + dx) % 4) * 2 + (y + dy) % 2
    order = [(0, 0), (3, 0), (1, 0), (0, 1), (3, 1), (2, 0), (1, 1), (2, 1)]
    features = jnp.stack([feature(dx, dy) for dx, dy in order]).astype(jnp.int32)
    chunks = tokens.reshape(16, CHUNKS, W, 1024)
    early, late = (chunks[:, j].reshape(ROWS, 1024) for j in range(CHUNKS))
    tables = []
    for j in range(CHUNKS):
        positions = old_mine[:, None] * FINE + j * W + jnp.arange(W, dtype=jnp.int32)[None, :]
        tables += angle_tables(positions.reshape(-1))
    old_flat = old_map.reshape(-1)

    left = shift_x(early, 1)
    right = shift_x(early, -1)
    across = swap_y(early)
    late, left, right, across, send_info, attend_info, old_flat, *tables = together(
        late, left, right, across, send_info, attend_info, old_flat, *tables
    )
    left_across = shift_x(across, 1)
    far = shift_x(right, -1)
    right_across = swap_y(right)
    late_across = swap_y(late)
    total = project(features[:4], [(early,), (left,), (right,), (across,)], weights)
    left_across, far, late = together(left_across, far, after(late, total))
    late_right = shift_x(late, -1)
    far_across = shift_x(left_across, 1)
    right_across = after(right_across, late)
    late_left = shift_x(after(late, right_across), 1)
    total = project(features[4:7], [(left_across,), (far,), (right_across,)], weights, total)
    late_right, late_across, total = together(late_right, late_across, total)
    late_far = shift_x(late_right, -1)
    late_right_across = swap_y(late_right)
    far_across = after(far_across, late_right)
    sent = project(features[7:], [(far_across,)], weights, total, (send_info, *tables[:2]), joint=True)
    partner = shift_ctx(sent[4], 1, 0)
    late_across, late_left = together(late_across, late_left, sent[0])[:2]
    late_left_across = shift_x(late_across, 1)
    blocks = [(late,), (late_left,), (late_right,), (late_across,)]
    total = project(features[:4], blocks, weights)
    late_far, late_right_across, total = together(late_far, late_right_across, total)
    late_far_across = shift_x(late_right_across, -1)
    early_parts = [
        jnp.concatenate([sent[dz], partner[:ROWS], partner[ROWS + dz * 4 * W : ROWS + (dz + 1) * 4 * W]], axis=0)
        for dz in range(4)
    ]
    *early_parts, total = together(*early_parts, total)
    total = project(features[5:7], [(late_far,), (late_right_across,)], weights, total)
    early_parts[1:] = [shift_ctx(early_parts[dz], 0, dz) for dz in range(1, 4)]
    last = jnp.stack([features[4], features[7]])
    tail = [(late_left_across,), (late_far_across,)]
    sent = project(last, tail, weights, total, (send_info, *tables[2:]))
    early_other = swap_core(jnp.concatenate(early_parts, axis=0))
    sent = list(sent)
    late_parts = [shift_ctx(sent[r], *CHIPS[r]) for r in range(4, 8)]
    early_parts[1], late_parts[0], *sent[:4] = together(early_parts[1], late_parts[0], *sent[:4])
    late_parts = [sent[0]] + [shift_ctx(sent[r], *CHIPS[r]) for r in range(1, 4)] + late_parts
    late_other = [swap_core(jnp.concatenate(late_parts[at : at + 4], axis=0)) for at in (0, 4)]
    return attend(attend_info, old_flat, [*early_parts, early_other, *late_parts, *late_other])


def solution(mesh):
    return jax.shard_map(
        local,
        mesh=mesh,
        in_specs=(P("ctx", "tp"), P(), P(), P(None, "tp"), P(None, "tp"), P(None, "tp")),
        out_specs=P("ctx", "tp"),
        check_vma=False,
    )
```

```python
import functools
import math

import jax
import jax.numpy as jnp
from jax import lax
from jax.experimental import pallas as pl
from jax.experimental.pallas import tpu as pltpu
from jax.sharding import PartitionSpec as P

HEAD = 128
THETA = 500000.0
SCALE = HEAD ** -0.5
LOG2E = math.log2(math.e)
FINE = 32
CHUNKS = 2
W = FINE // CHUNKS
ROWS = 16 * W
PAYLOAD = 20 * W
KB = 512
VMEM = pl.BlockSpec(memory_space=pltpu.VMEM)
SMEM = pl.BlockSpec(memory_space=pltpu.SMEM)
ANY = pl.BlockSpec(memory_space=pl.ANY)

CHIPS = [(dh, dz) for dh in range(2) for dz in range(4)]


def shift_x(block, step):
    perm = [(i * 2 + j, ((i + step) % 4) * 2 + j) for i in range(4) for j in range(2)]
    return lax.ppermute(block, "tp", perm)


def swap_y(block):
    return lax.ppermute(block, "tp", [(i, i ^ 1) for i in range(8)])


def shift_ctx(block, dh, dz):
    perm = [
        (h * 8 + z * 2 + c, (h ^ dh) * 8 + ((z + dz) % 4) * 2 + c)
        for h in range(2)
        for z in range(4)
        for c in range(2)
    ]
    return lax.ppermute(block, "ctx", perm)


def together(*values):
    return lax.optimization_barrier(values)


def after(value, *others):
    return lax.optimization_barrier((value, *others))[0]


def swap_core(block):
    return lax.ppermute(block, "ctx", [(i, i ^ 1) for i in range(16)])


def dot(a, b):
    return lax.dot_general(a, b, (((1,), (0,)), ((), ())), preferred_element_type=jnp.float32)


def dot_t(a, b):
    return lax.dot_general(a, b, (((1,), (1,)), ((), ())), preferred_element_type=jnp.float32)


def fold(block, combine):
    result = block[:, :HEAD]
    for at in range(HEAD, block.shape[1], HEAD):
        result = combine(result, block[:, at : at + HEAD])
    return result


def less(block, lanes):
    return jnp.concatenate([block[:, at : at + HEAD] - lanes for at in range(0, block.shape[1], HEAD)], axis=1)


def project_kernel(count, has_acc, last, joint, features, *refs):
    blocks, (wq, wk, wv), refs = refs[:count], refs[count : count + 3], refs[count + 3 :]
    acc_in = None
    if has_acc:
        acc_in, refs = refs[0], refs[1:]
    if last:
        info, cosine, sine = refs[:3]
        held, held_sems, acc, heads, packed, packed_sems = refs[-6:]
        outs = refs[3:-6]
    else:
        acc, held, held_sems = refs
    copies = [pltpu.make_async_copy(blocks[i], held.at[i], held_sems.at[i]) for i in range(count)]
    for copy in copies:
        copy.start()
    for i, copy in enumerate(copies):
        copy.wait()
        rows = pl.ds(pl.multiple_of(features[i] * 1024, 1024), 1024)
        block = held[i]
        for lo, hi in ((0, 512), (512, 768)):
            w = wq[rows, :] if lo == 0 else jnp.concatenate([wk[rows, :], wv[rows, :]], axis=1)
            value = dot(block, w)
            if i > 0:
                value = value + acc[:, lo:hi]
            elif has_acc:
                value = value + acc_in[:, lo:hi]
            acc[:, lo:hi] = value
    if not last:
        return
    cos, sin = cosine[...], sine[...]

    def rotated(lo):
        vector = acc[:, lo : lo + HEAD]
        return (vector * cos + pltpu.roll(vector, HEAD // 2, 1) * sin).astype(jnp.bfloat16)

    for h in range(4):
        heads[:, h * HEAD : (h + 1) * HEAD] = rotated(h * HEAD)
    key = rotated(512)
    value = acc[:, 640:768].astype(jnp.bfloat16)
    me = info[0]
    high, z = me // 8, lax.rem(me // 2, 4)
    starts = [sum(out.shape[0] for out in outs[:r]) for r in range(len(outs))]
    sends = []
    for r, out in enumerate(outs):
        base = starts[r]
        packed[base : base + ROWS, 0:HEAD] = key
        packed[base : base + ROWS, HEAD : 2 * HEAD] = value
        chips = CHIPS[4:] if joint and r == 4 else CHIPS[r : r + 1]
        for n, (dh, dz) in enumerate(chips):
            chip = lax.rem(high + dh, 2) * 8 + lax.rem(z + dz, 4) * 2
            for core in range(2):
                rows = pl.ds(pl.multiple_of(info[1 + chip + core] * W, W), W)
                for half in range(2):
                    at = base + ROWS + (n * 4 + core * 2 + half) * W
                    packed[at : at + W, :] = heads[rows, half * 256 : half * 256 + 256]
        send = pltpu.make_async_copy(packed.at[base : base + out.shape[0]], out, packed_sems.at[r])
        send.start()
        sends.append(send)
    for send in sends:
        send.wait()


def project(features, blocks, weights, acc=None, tables=None, joint=False):
    count = len(blocks)
    last = tables is not None
    specs = [SMEM] + [ANY] * count + [VMEM] * 3
    operands = [features, *blocks, *weights]
    if acc is not None:
        specs.append(VMEM)
        operands.append(acc)
    scratch = [pltpu.VMEM((count, ROWS, 1024), jnp.bfloat16), pltpu.SemaphoreType.DMA((count,))]
    if last:
        specs += [SMEM, VMEM, VMEM]
        operands += list(tables)
        sizes = [PAYLOAD] * 4 + [2 * ROWS] if joint else [PAYLOAD] * 8
        out_shape = [jax.ShapeDtypeStruct((n, 256), jnp.bfloat16) for n in sizes]
        out_specs = [ANY] * len(sizes)
        scratch += [
            pltpu.VMEM((ROWS, 768), jnp.float32),
            pltpu.VMEM((ROWS, 512), jnp.bfloat16),
            pltpu.VMEM((sum(sizes), 256), jnp.bfloat16),
            pltpu.SemaphoreType.DMA((len(sizes),)),
        ]
    else:
        out_shape = jax.ShapeDtypeStruct((ROWS, 768), jnp.float32)
        out_specs = VMEM
    return pl.pallas_call(
        functools.partial(project_kernel, count, acc is not None, last, joint),
        in_specs=specs,
        out_specs=out_specs,
        out_shape=out_shape,
        scratch_shapes=scratch,
        compiler_params=pltpu.CompilerParams(vmem_limit_bytes=32 * 2**20),
        cost_estimate=pl.CostEstimate(flops=1, bytes_accessed=1, transcendentals=0),
        name="project",
    )(*operands)


def attend_kernel(info, old_map, *refs):
    packed, packed_other, late, late_other = refs[:4], refs[4], refs[5:13], refs[13:15]
    out, query, keys, values, top, total, accum = refs[15:]
    me = info[0]
    high, z, core = me // 8, lax.rem(me // 2, 4), lax.rem(me, 2)
    for r, (dh, dz) in enumerate(CHIPS):
        for swapped in range(2):
            source = lax.rem(high + dh, 2) * 8 + lax.rem(z + 4 - dz, 4) * 2 + lax.rem(core + swapped, 2)
            slot = info[3 + source]
            for j in range(CHUNKS):
                if j == 0:
                    ref, base = (packed_other, (dz * 2 + dh) * PAYLOAD) if swapped else (packed[dz], dh * PAYLOAD)
                else:
                    ref, base = (late_other[r // 4], (r % 4) * PAYLOAD) if swapped else (late[r], 0)
                for k in range(16):
                    at = pl.ds(pl.multiple_of(old_map[source * 16 + k] * FINE + j * W, W), W)
                    rows = slice(base + k * W, base + (k + 1) * W)
                    keys[at, :] = ref[rows, 0:HEAD]
                    values[at, :] = ref[rows, HEAD : 2 * HEAD]
                for h in range(4):
                    at = pl.ds(pl.multiple_of(base + ROWS + (core * 2 + h // 2) * W, W), W)
                    to = (slot // 8) * 1024 + h * 256 + lax.rem(slot, 8) * FINE + j * W
                    query[pl.ds(pl.multiple_of(to, W), W), :] = ref[at, (h % 2) * HEAD : (h % 2 + 1) * HEAD]

    for u in range(2):
        coarse = info[1 + u]
        queries = query[u * 1024 : (u + 1) * 1024, :]
        top[...] = jnp.full(top.shape, -1e30, jnp.float32)
        total[...] = jnp.zeros_like(total)
        accum[...] = jnp.zeros_like(accum)
        whole = (coarse * 256) // KB

        def absorb(block, masked, coarse=coarse, queries=queries):
            start = pl.multiple_of(block * KB, KB)
            scores = dot_t(queries, keys[pl.ds(start, KB), :])
            if masked:
                row = lax.rem(lax.broadcasted_iota(jnp.int32, (1024, KB), 0), 256) + coarse * 256
                visible = lax.broadcasted_iota(jnp.int32, (1024, KB), 1) + start <= row
                scores = jnp.where(visible, scores, -1e30)
            old = top[...]
            new = jnp.maximum(old, jnp.max(fold(scores, jnp.maximum), axis=-1, keepdims=True))
            factor = jnp.exp2((old - new) * (SCALE * LOG2E))
            weights = jnp.exp2(less(scores, new) * (SCALE * LOG2E))
            if masked:
                weights = jnp.where(visible, weights, 0.0)
            total[...] = total[...] * factor + fold(weights, jnp.add)
            accum[...] = accum[...] * factor + dot(
                weights.astype(jnp.bfloat16), values[pl.ds(start, KB), :]
            )
            top[...] = new

        def body(block, carry, absorb=absorb):
            absorb(block, False)
            return carry

        lax.fori_loop(0, whole, body, 0)
        absorb(whole, True)
        result = accum[...] / jnp.sum(total[...], axis=-1, keepdims=True)
        for h in range(4):
            out[u * 256 : (u + 1) * 256, h * HEAD : (h + 1) * HEAD] = result[h * 256 : (h + 1) * 256].astype(
                jnp.bfloat16
            )


def attend(info, old_map, parts):
    return pl.pallas_call(
        attend_kernel,
        out_shape=jax.ShapeDtypeStruct((512, 512), jnp.bfloat16),
        in_specs=[SMEM, SMEM] + [VMEM] * len(parts),
        out_specs=VMEM,
        scratch_shapes=[
            pltpu.VMEM((2048, HEAD), jnp.bfloat16),
            pltpu.VMEM((8192, HEAD), jnp.bfloat16),
            pltpu.VMEM((8192, HEAD), jnp.bfloat16),
            pltpu.VMEM((1024, HEAD), jnp.float32),
            pltpu.VMEM((1024, HEAD), jnp.float32),
            pltpu.VMEM((1024, HEAD), jnp.float32),
        ],
        compiler_params=pltpu.CompilerParams(vmem_limit_bytes=56 * 2**20),
        name="attend",
    )(info, old_map, *parts)


def routing(old_map, new_map, own_index):
    devices = jnp.arange(16, dtype=jnp.int32)
    old_mine = lax.dynamic_index_in_dim(old_map, own_index, 0, keepdims=False)
    new_mine = lax.dynamic_index_in_dim(new_map, own_index, 0, keepdims=False)
    outward = jnp.any(new_map[:, :, None] == old_mine[None, None, :], axis=1)
    send_order = jnp.sum(outward.astype(jnp.int32) * devices[None, :], axis=1)
    inward = jnp.any(old_map[:, :, None] == new_mine[None, None, :], axis=1)
    slot_of = jnp.sum(inward.astype(jnp.int32) * devices[None, :], axis=1)
    coarse = jnp.stack([new_mine[0] // 8, new_mine[8] // 8])
    return (
        jnp.concatenate([own_index[None], send_order]).astype(jnp.int32),
        jnp.concatenate([own_index[None], coarse, slot_of]).astype(jnp.int32),
        old_mine,
    )


def angle_tables(positions):
    half = HEAD // 2
    freqs = jnp.exp(jnp.arange(half, dtype=jnp.float32) * (-2.0 * math.log(THETA) / HEAD))
    angles = positions.astype(jnp.float32)[:, None] * freqs[None, :]
    cosine = jnp.cos(angles)
    sine = jnp.sin(angles)
    return jnp.concatenate([cosine, cosine], axis=1), jnp.concatenate([-sine, sine], axis=1)


def local(tokens, old_map, new_map, w_query, key_projection_weight, value_projection_weight):
    me = lax.axis_index("ctx").astype(jnp.int32)
    place = lax.axis_index("tp").astype(jnp.int32)
    weights = (w_query, key_projection_weight, value_projection_weight)
    send_info, attend_info, old_mine = routing(old_map, new_map, me)
    x, y = place // 2, place % 2
    feature = lambda dx, dy: ((x + dx) % 4) * 2 + (y + dy) % 2
    order = [(0, 0), (3, 0), (1, 0), (0, 1), (3, 1), (2, 0), (1, 1), (2, 1)]
    features = jnp.stack([feature(dx, dy) for dx, dy in order]).astype(jnp.int32)
    chunks = tokens.reshape(16, CHUNKS, W, 1024)
    early, late = (chunks[:, j].reshape(ROWS, 1024) for j in range(CHUNKS))
    tables = []
    for j in range(CHUNKS):
        positions = old_mine[:, None] * FINE + j * W + jnp.arange(W, dtype=jnp.int32)[None, :]
        tables += angle_tables(positions.reshape(-1))
    old_flat = old_map.reshape(-1)

    left = shift_x(early, 1)
    right = shift_x(early, -1)
    across = swap_y(early)
    late, left, right, across, send_info, attend_info, old_flat, *tables = together(
        late, left, right, across, send_info, attend_info, old_flat, *tables
    )
    left_across = shift_x(across, 1)
    far = shift_x(right, -1)
    right_across = swap_y(right)
    late_across = swap_y(late)
    total = project(features[:4], [early, left, right, across], weights)
    left_across, far, late = together(left_across, far, after(late, total))
    late_right = shift_x(late, -1)
    far_across = shift_x(left_across, 1)
    right_across = after(right_across, late)
    total = project(features[4:7], [left_across, far, right_across], weights, total)
    late_right, total = together(late_right, total)
    late_far = shift_x(late_right, -1)
    late_right_across = swap_y(late_right)
    far_across = after(far_across, late_right)
    late_left = shift_x(after(late, far_across), 1)
    sent = project(features[7:], [far_across], weights, total, (send_info, *tables[:2]), joint=True)
    partner = shift_ctx(sent[4], 1, 0)
    late_across, late_left = together(late_across, late_left, sent[0])[:2]
    late_left_across = shift_x(late_across, 1)
    total = project(features[:4], [late, late_left, late_right, late_across], weights)
    late_far, late_right_across = together(late_far, late_right_across)
    late_far_across = shift_x(late_right_across, -1)
    partner, total = together(partner, total)
    early_parts = [
        jnp.concatenate([sent[dz], partner[:ROWS], partner[ROWS + dz * 4 * W : ROWS + (dz + 1) * 4 * W]], axis=0)
        for dz in range(4)
    ]
    *early_parts, total = together(*early_parts, total)
    total = project(features[5:7], [late_far, late_right_across], weights, total)
    early_parts[1:] = [shift_ctx(early_parts[dz], 0, dz) for dz in range(1, 4)]
    last = jnp.stack([features[4], features[7]])
    tail = [late_left_across, late_far_across]
    sent = project(last, tail, weights, total, (send_info, *tables[2:]))
    early_other = swap_core(jnp.concatenate(early_parts, axis=0))
    sent = list(sent)
    late_parts = [shift_ctx(sent[r], *CHIPS[r]) for r in range(4, 8)]
    early_parts[1], late_parts[0], *sent[:4] = together(early_parts[1], late_parts[0], *sent[:4])
    late_parts = [sent[0]] + [shift_ctx(sent[r], *CHIPS[r]) for r in range(1, 4)] + late_parts
    late_other = [swap_core(jnp.concatenate(late_parts[at : at + 4], axis=0)) for at in (0, 4)]
    return attend(attend_info, old_flat, [*early_parts, early_other, *late_parts, *late_other])


def solution(mesh):
    return jax.shard_map(
        local,
        mesh=mesh,
        in_specs=(P("ctx", "tp"), P(), P(), P(None, "tp"), P(None, "tp"), P(None, "tp")),
        out_specs=P("ctx", "tp"),
        check_vma=False,
    )
```

```python
import functools
import math

import jax
import jax.numpy as jnp
from jax import lax
from jax.experimental import pallas as pl
from jax.experimental.pallas import tpu as pltpu
from jax.sharding import PartitionSpec as P

HEAD = 128
THETA = 500000.0
SCALE = HEAD ** -0.5
LOG2E = math.log2(math.e)
FINE = 32
CHUNKS = 2
W = FINE // CHUNKS
ROWS = 16 * W
PAYLOAD = 20 * W
KB = 512
VMEM = pl.BlockSpec(memory_space=pltpu.VMEM)
SMEM = pl.BlockSpec(memory_space=pltpu.SMEM)
HBM = pl.BlockSpec(memory_space=pltpu.HBM)

CHIPS = [(dh, dz) for dh in range(2) for dz in range(4)]


def shift_x(block, step):
    perm = [(i * 2 + j, ((i + step) % 4) * 2 + j) for i in range(4) for j in range(2)]
    return lax.ppermute(block, "tp", perm)


def swap_y(block):
    return lax.ppermute(block, "tp", [(i, i ^ 1) for i in range(8)])


def shift_ctx(block, dh, dz):
    perm = [
        (h * 8 + z * 2 + c, (h ^ dh) * 8 + ((z + dz) % 4) * 2 + c)
        for h in range(2)
        for z in range(4)
        for c in range(2)
    ]
    return lax.ppermute(block, "ctx", perm)


def together(*values):
    return lax.optimization_barrier(values)


def after(value, *others):
    return lax.optimization_barrier((value, *others))[0]


def swap_core(block):
    return lax.ppermute(block, "ctx", [(i, i ^ 1) for i in range(16)])


def dot(a, b):
    return lax.dot_general(a, b, (((1,), (0,)), ((), ())), preferred_element_type=jnp.float32)


def dot_t(a, b):
    return lax.dot_general(a, b, (((1,), (1,)), ((), ())), preferred_element_type=jnp.float32)


def fold(block, combine):
    result = block[:, :HEAD]
    for at in range(HEAD, block.shape[1], HEAD):
        result = combine(result, block[:, at : at + HEAD])
    return result


def less(block, lanes):
    return jnp.concatenate([block[:, at : at + HEAD] - lanes for at in range(0, block.shape[1], HEAD)], axis=1)


def project_kernel(count, has_acc, last, joint, features, *refs):
    blocks, weights, refs = refs[:count], refs[count], refs[count + 1 :]
    acc_in = None
    if has_acc:
        acc_in, refs = refs[0], refs[1:]
    if last:
        info, cosine, sine = refs[:3]
        held, held_sems, acc, heads, packed, packed_sems = refs[-6:]
        outs = refs[3:-6]
    else:
        acc, held, held_sems = refs
    copies = [pltpu.make_async_copy(blocks[i], held.at[i], held_sems.at[i]) for i in range(count)]
    for copy in copies:
        copy.start()
    for i, copy in enumerate(copies):
        copy.wait()
        rows = pl.ds(pl.multiple_of(features[i] * 1024, 1024), 1024)
        block = held[i]
        value = dot(block, weights[rows, :])
        if i > 0:
            value = value + acc[...]
        elif has_acc:
            value = value + acc_in[...]
        acc[...] = value
    if not last:
        return
    cos, sin = cosine[...], sine[...]

    def rotated(lo):
        vector = acc[:, lo : lo + HEAD]
        return (vector * cos + pltpu.roll(vector, HEAD // 2, 1) * sin).astype(jnp.bfloat16)

    for h in range(4):
        heads[:, h * HEAD : (h + 1) * HEAD] = rotated(h * HEAD)
    key = rotated(512)
    value = acc[:, 640:768].astype(jnp.bfloat16)
    me = info[0]
    high, z = me // 8, lax.rem(me // 2, 4)
    starts = [sum(out.shape[0] for out in outs[:r]) for r in range(len(outs))]
    sends = []
    for r, out in enumerate(outs):
        base = starts[r]
        packed[base : base + ROWS, 0:HEAD] = key
        packed[base : base + ROWS, HEAD : 2 * HEAD] = value
        chips = CHIPS[4:] if joint and r == 4 else CHIPS[r : r + 1]
        for n, (dh, dz) in enumerate(chips):
            chip = lax.rem(high + dh, 2) * 8 + lax.rem(z + dz, 4) * 2
            for core in range(2):
                rows = pl.ds(pl.multiple_of(info[1 + chip + core] * W, W), W)
                for half in range(2):
                    at = base + ROWS + (n * 4 + core * 2 + half) * W
                    packed[at : at + W, :] = heads[rows, half * 256 : half * 256 + 256]
        send = pltpu.make_async_copy(packed.at[base : base + out.shape[0]], out, packed_sems.at[r])
        send.start()
        sends.append(send)
    for send in sends:
        send.wait()


def project(features, blocks, weights, acc=None, tables=None, joint=False):
    count = len(blocks)
    last = tables is not None
    specs = [SMEM] + [HBM] * count + [VMEM]
    operands = [features, *blocks, weights]
    if acc is not None:
        specs.append(VMEM)
        operands.append(acc)
    scratch = [pltpu.VMEM((count, ROWS, 1024), jnp.bfloat16), pltpu.SemaphoreType.DMA((count,))]
    if last:
        specs += [SMEM, VMEM, VMEM]
        operands += list(tables)
        sizes = [PAYLOAD] * 4 + [2 * ROWS] if joint else [PAYLOAD] * 8
        out_shape = [jax.ShapeDtypeStruct((n, 256), jnp.bfloat16) for n in sizes]
        out_specs = [HBM] * len(sizes)
        scratch += [
            pltpu.VMEM((ROWS, 768), jnp.float32),
            pltpu.VMEM((ROWS, 512), jnp.bfloat16),
            pltpu.VMEM((sum(sizes), 256), jnp.bfloat16),
            pltpu.SemaphoreType.DMA((len(sizes),)),
        ]
    else:
        out_shape = jax.ShapeDtypeStruct((ROWS, 768), jnp.float32)
        out_specs = VMEM
    return pl.pallas_call(
        functools.partial(project_kernel, count, acc is not None, last, joint),
        in_specs=specs,
        out_specs=out_specs,
        out_shape=out_shape,
        scratch_shapes=scratch,
        compiler_params=pltpu.CompilerParams(vmem_limit_bytes=32 * 2**20),
        cost_estimate=pl.CostEstimate(flops=1, bytes_accessed=1, transcendentals=0),
        name="project",
    )(*operands)


def attend_kernel(info, old_map, *refs):
    packed, packed_other, late, late_source = refs[:4], refs[4], refs[5:13], refs[13:15]
    out, query, keys, values, top, total, accum, late_other, sems = refs[15:]
    copies = [pltpu.make_async_copy(late_source[i], late_other.at[i], sems.at[i]) for i in range(2)]
    for copy in copies:
        copy.start()
    me = info[0]
    high, z, core = me // 8, lax.rem(me // 2, 4), lax.rem(me, 2)
    for swapped in range(2):
        for r, (dh, dz) in enumerate(CHIPS):
            if swapped and r % 4 == 0:
                copies[r // 4].wait()
            source = lax.rem(high + dh, 2) * 8 + lax.rem(z + 4 - dz, 4) * 2 + lax.rem(core + swapped, 2)
            slot = info[3 + source]
            for j in range(CHUNKS):
                if j == 0:
                    ref, base = (packed_other, (dz * 2 + dh) * PAYLOAD) if swapped else (packed[dz], dh * PAYLOAD)
                else:
                    ref, base = (late_other.at[r // 4], (r % 4) * PAYLOAD) if swapped else (late[r], 0)
                for k in range(16):
                    at = pl.ds(pl.multiple_of(old_map[source * 16 + k] * FINE + j * W, W), W)
                    rows = slice(base + k * W, base + (k + 1) * W)
                    keys[at, :] = ref[rows, 0:HEAD]
                    values[at, :] = ref[rows, HEAD : 2 * HEAD]
                for h in range(4):
                    at = pl.ds(pl.multiple_of(base + ROWS + (core * 2 + h // 2) * W, W), W)
                    to = (slot // 8) * 1024 + h * 256 + lax.rem(slot, 8) * FINE + j * W
                    query[pl.ds(pl.multiple_of(to, W), W), :] = ref[at, (h % 2) * HEAD : (h % 2 + 1) * HEAD]

    for u in range(2):
        coarse = info[1 + u]
        queries = query[u * 1024 : (u + 1) * 1024, :]
        top[...] = jnp.full(top.shape, -1e30, jnp.float32)
        total[...] = jnp.zeros_like(total)
        accum[...] = jnp.zeros_like(accum)
        whole = (coarse * 256) // KB

        def absorb(block, masked, coarse=coarse, queries=queries):
            start = pl.multiple_of(block * KB, KB)
            scores = dot_t(queries, keys[pl.ds(start, KB), :])
            if masked:
                row = lax.rem(lax.broadcasted_iota(jnp.int32, (1024, KB), 0), 256) + coarse * 256
                visible = lax.broadcasted_iota(jnp.int32, (1024, KB), 1) + start <= row
                scores = jnp.where(visible, scores, -1e30)
            old = top[...]
            new = jnp.maximum(old, jnp.max(fold(scores, jnp.maximum), axis=-1, keepdims=True))
            factor = jnp.exp2((old - new) * (SCALE * LOG2E))
            weights = jnp.exp2(less(scores, new) * (SCALE * LOG2E))
            if masked:
                weights = jnp.where(visible, weights, 0.0)
            total[...] = total[...] * factor + fold(weights, jnp.add)
            accum[...] = accum[...] * factor + dot(
                weights.astype(jnp.bfloat16), values[pl.ds(start, KB), :]
            )
            top[...] = new

        def body(block, carry, absorb=absorb):
            absorb(block, False)
            return carry

        lax.fori_loop(0, whole, body, 0)
        absorb(whole, True)
        result = accum[...] / jnp.sum(total[...], axis=-1, keepdims=True)
        for h in range(4):
            out[u * 256 : (u + 1) * 256, h * HEAD : (h + 1) * HEAD] = result[h * 256 : (h + 1) * 256].astype(
                jnp.bfloat16
            )


def attend(info, old_map, parts):
    return pl.pallas_call(
        attend_kernel,
        out_shape=jax.ShapeDtypeStruct((512, 512), jnp.bfloat16),
        in_specs=[SMEM, SMEM] + [VMEM] * (len(parts) - 2) + [HBM] * 2,
        out_specs=VMEM,
        scratch_shapes=[
            pltpu.VMEM((2048, HEAD), jnp.bfloat16),
            pltpu.VMEM((8192, HEAD), jnp.bfloat16),
            pltpu.VMEM((8192, HEAD), jnp.bfloat16),
            pltpu.VMEM((1024, HEAD), jnp.float32),
            pltpu.VMEM((1024, HEAD), jnp.float32),
            pltpu.VMEM((1024, HEAD), jnp.float32),
            pltpu.VMEM((2, 4 * PAYLOAD, 256), jnp.bfloat16),
            pltpu.SemaphoreType.DMA((2,)),
        ],
        compiler_params=pltpu.CompilerParams(vmem_limit_bytes=56 * 2**20),
        name="attend",
    )(info, old_map, *parts)


def routing(old_map, new_map, own_index):
    devices = jnp.arange(16, dtype=jnp.int32)
    old_mine = lax.dynamic_index_in_dim(old_map, own_index, 0, keepdims=False)
    new_mine = lax.dynamic_index_in_dim(new_map, own_index, 0, keepdims=False)
    outward = jnp.any(new_map[:, :, None] == old_mine[None, None, :], axis=1)
    send_order = jnp.sum(outward.astype(jnp.int32) * devices[None, :], axis=1)
    inward = jnp.any(old_map[:, :, None] == new_mine[None, None, :], axis=1)
    slot_of = jnp.sum(inward.astype(jnp.int32) * devices[None, :], axis=1)
    coarse = jnp.stack([new_mine[0] // 8, new_mine[8] // 8])
    return (
        jnp.concatenate([own_index[None], send_order]).astype(jnp.int32),
        jnp.concatenate([own_index[None], coarse, slot_of]).astype(jnp.int32),
        old_mine,
    )


def angle_tables(positions):
    half = HEAD // 2
    freqs = jnp.exp(jnp.arange(half, dtype=jnp.float32) * (-2.0 * math.log(THETA) / HEAD))
    angles = positions.astype(jnp.float32)[:, None] * freqs[None, :]
    cosine = jnp.cos(angles)
    sine = jnp.sin(angles)
    return jnp.concatenate([cosine, cosine], axis=1), jnp.concatenate([-sine, sine], axis=1)


def local(tokens, old_map, new_map, w_query, key_projection_weight, value_projection_weight):
    me = lax.axis_index("ctx").astype(jnp.int32)
    place = lax.axis_index("tp").astype(jnp.int32)
    weights = jnp.concatenate([w_query, key_projection_weight, value_projection_weight], axis=1)
    send_info, attend_info, old_mine = routing(old_map, new_map, me)
    x, y = place // 2, place % 2
    feature = lambda dx, dy: ((x + dx) % 4) * 2 + (y + dy) % 2
    order = [(0, 0), (3, 0), (1, 0), (0, 1), (3, 1), (2, 0), (1, 1), (2, 1)]
    features = jnp.stack([feature(dx, dy) for dx, dy in order]).astype(jnp.int32)
    chunks = tokens.reshape(16, CHUNKS, W, 1024)
    early, late = (chunks[:, j].reshape(ROWS, 1024) for j in range(CHUNKS))
    tables = []
    for j in range(CHUNKS):
        positions = old_mine[:, None] * FINE + j * W + jnp.arange(W, dtype=jnp.int32)[None, :]
        tables += angle_tables(positions.reshape(-1))
    old_flat = old_map.reshape(-1)

    left = shift_x(early, 1)
    right = shift_x(early, -1)
    across = swap_y(early)
    weights, late, left, right, across, send_info, attend_info, old_flat, *tables = together(
        weights, late, left, right, across, send_info, attend_info, old_flat, *tables
    )
    left_across = shift_x(across, 1)
    far = shift_x(right, -1)
    right_across = swap_y(right)
    late_across = swap_y(late)
    total = project(features[:4], [early, left, right, across], weights)
    left_across, far, late = together(left_across, far, after(late, total))
    late_right = shift_x(late, -1)
    far_across = shift_x(left_across, 1)
    right_across = after(right_across, late)
    total = project(features[4:7], [left_across, far, right_across], weights, total)
    late_right, total = together(late_right, total)
    late_far = shift_x(late_right, -1)
    late_right_across = swap_y(late_right)
    far_across = after(far_across, late_right)
    late_left = shift_x(after(late, far_across), 1)
    sent = project(features[7:], [far_across], weights, total, (send_info, *tables[:2]), joint=True)
    partner = shift_ctx(sent[4], 1, 0)
    late_across, late_left = together(late_across, late_left, sent[0])[:2]
    late_left_across = shift_x(late_across, 1)
    total = project(features[:4], [late, late_left, late_right, late_across], weights)
    late_far, late_right_across = together(late_far, late_right_across)
    late_far_across = shift_x(late_right_across, -1)
    partner, total = together(partner, total)
    early_parts = [
        jnp.concatenate([sent[dz], partner[:ROWS], partner[ROWS + dz * 4 * W : ROWS + (dz + 1) * 4 * W]], axis=0)
        for dz in range(4)
    ]
    *early_parts, total = together(*early_parts, total)
    total = project(features[5:7], [late_far, late_right_across], weights, total)
    early_parts[1:] = [shift_ctx(early_parts[dz], 0, dz) for dz in range(1, 4)]
    last = jnp.stack([features[4], features[7]])
    tail = [late_left_across, late_far_across]
    sent = project(last, tail, weights, total, (send_info, *tables[2:]))
    early_other = swap_core(jnp.concatenate(early_parts, axis=0))
    sent = list(sent)
    late_parts = [shift_ctx(sent[r], *CHIPS[r]) for r in range(4, 8)]
    early_parts[1], late_parts[0], *sent[:4] = together(early_parts[1], late_parts[0], *sent[:4])
    late_parts = [sent[0]] + [shift_ctx(sent[r], *CHIPS[r]) for r in range(1, 4)] + late_parts
    late_other = [swap_core(jnp.concatenate(late_parts[at : at + 4], axis=0)) for at in (0, 4)]
    return attend(attend_info, old_flat, [*early_parts, early_other, *late_parts, *late_other])


def solution(mesh):
    return jax.shard_map(
        local,
        mesh=mesh,
        in_specs=(P("ctx", "tp"), P(), P(), P(None, "tp"), P(None, "tp"), P(None, "tp")),
        out_specs=P("ctx", "tp"),
        check_vma=False,
    )
```

```python
import functools
import math

import jax
import jax.numpy as jnp
from jax import lax
from jax.experimental import pallas as pl
from jax.experimental.pallas import tpu as pltpu
from jax.sharding import PartitionSpec as P

HEAD = 128
THETA = 500000.0
SCALE = HEAD ** -0.5
LOG2E = math.log2(math.e)
FINE = 32
CHUNKS = 2
W = FINE // CHUNKS
ROWS = 16 * W
PAYLOAD = 20 * W
KB = 512
VMEM = pl.BlockSpec(memory_space=pltpu.VMEM)
SMEM = pl.BlockSpec(memory_space=pltpu.SMEM)
HBM = pl.BlockSpec(memory_space=pltpu.HBM)

CHIPS = [(dh, dz) for dh in range(2) for dz in range(4)]


def shift_x(block, step):
    perm = [(i * 2 + j, ((i + step) % 4) * 2 + j) for i in range(4) for j in range(2)]
    return lax.ppermute(block, "tp", perm)


def swap_y(block):
    return lax.ppermute(block, "tp", [(i, i ^ 1) for i in range(8)])


def shift_ctx(block, dh, dz):
    perm = [
        (h * 8 + z * 2 + c, (h ^ dh) * 8 + ((z + dz) % 4) * 2 + c)
        for h in range(2)
        for z in range(4)
        for c in range(2)
    ]
    return lax.ppermute(block, "ctx", perm)


def together(*values):
    return lax.optimization_barrier(values)


def after(value, *others):
    return lax.optimization_barrier((value, *others))[0]


def swap_core(block):
    return lax.ppermute(block, "ctx", [(i, i ^ 1) for i in range(16)])


def dot(a, b):
    return lax.dot_general(a, b, (((1,), (0,)), ((), ())), preferred_element_type=jnp.float32)


def dot_t(a, b):
    return lax.dot_general(a, b, (((1,), (1,)), ((), ())), preferred_element_type=jnp.float32)


def fold(block, combine):
    result = block[:, :HEAD]
    for at in range(HEAD, block.shape[1], HEAD):
        result = combine(result, block[:, at : at + HEAD])
    return result


def less(block, lanes):
    return jnp.concatenate([block[:, at : at + HEAD] - lanes for at in range(0, block.shape[1], HEAD)], axis=1)


def project_kernel(count, has_acc, last, joint, features, *refs):
    blocks, weights, refs = refs[:count], refs[count : count + 3], refs[count + 3 :]
    acc_in = None
    if has_acc:
        acc_in, refs = refs[0], refs[1:]
    if last:
        info, cosine, sine = refs[:3]
        held, joined, held_sems, acc, heads, packed, packed_sems = refs[-7:]
        outs = refs[3:-7]
    else:
        acc, held, joined, held_sems = refs
    copies = []
    for i in range(count):
        rows = pl.ds(pl.multiple_of(features[i] * 1024, 1024), 1024)
        pairs = [(blocks[i], held.at[i])]
        for w, lo in zip(weights, (0, 512, 640)):
            pairs.append((w.at[rows, :], joined.at[i, :, lo : lo + w.shape[1]]))
        copies.append([pltpu.make_async_copy(a, b, held_sems.at[i, n]) for n, (a, b) in enumerate(pairs)])
        for copy in copies[i]:
            copy.start()
    for i in range(count):
        for copy in copies[i]:
            copy.wait()
        value = dot(held[i], joined[i])
        if i > 0:
            value = value + acc[...]
        elif has_acc:
            value = value + acc_in[...]
        acc[...] = value
    if not last:
        return
    cos, sin = cosine[...], sine[...]

    def rotated(lo):
        vector = acc[:, lo : lo + HEAD]
        return (vector * cos + pltpu.roll(vector, HEAD // 2, 1) * sin).astype(jnp.bfloat16)

    for h in range(4):
        heads[:, h * HEAD : (h + 1) * HEAD] = rotated(h * HEAD)
    key = rotated(512)
    value = acc[:, 640:768].astype(jnp.bfloat16)
    me = info[0]
    high, z = me // 8, lax.rem(me // 2, 4)
    starts = [sum(out.shape[0] for out in outs[:r]) for r in range(len(outs))]
    sends = []
    for r, out in enumerate(outs):
        base = starts[r]
        packed[base : base + ROWS, 0:HEAD] = key
        packed[base : base + ROWS, HEAD : 2 * HEAD] = value
        chips = CHIPS[4:] if joint and r == 4 else CHIPS[r : r + 1]
        for n, (dh, dz) in enumerate(chips):
            chip = lax.rem(high + dh, 2) * 8 + lax.rem(z + dz, 4) * 2
            for core in range(2):
                rows = pl.ds(pl.multiple_of(info[1 + chip + core] * W, W), W)
                for half in range(2):
                    at = base + ROWS + (n * 4 + core * 2 + half) * W
                    packed[at : at + W, :] = heads[rows, half * 256 : half * 256 + 256]
        send = pltpu.make_async_copy(packed.at[base : base + out.shape[0]], out, packed_sems.at[r])
        send.start()
        sends.append(send)
    for send in sends:
        send.wait()


def project(features, blocks, weights, acc=None, tables=None, joint=False):
    count = len(blocks)
    last = tables is not None
    specs = [SMEM] + [HBM] * (count + 3)
    operands = [features, *blocks, *weights]
    if acc is not None:
        specs.append(VMEM)
        operands.append(acc)
    scratch = [
        pltpu.VMEM((count, ROWS, 1024), jnp.bfloat16),
        pltpu.VMEM((count, 1024, 768), jnp.bfloat16),
        pltpu.SemaphoreType.DMA((count, 4)),
    ]
    if last:
        specs += [SMEM, VMEM, VMEM]
        operands += list(tables)
        sizes = [PAYLOAD] * 4 + [2 * ROWS] if joint else [PAYLOAD] * 8
        out_shape = [jax.ShapeDtypeStruct((n, 256), jnp.bfloat16) for n in sizes]
        out_specs = [HBM] * len(sizes)
        scratch += [
            pltpu.VMEM((ROWS, 768), jnp.float32),
            pltpu.VMEM((ROWS, 512), jnp.bfloat16),
            pltpu.VMEM((sum(sizes), 256), jnp.bfloat16),
            pltpu.SemaphoreType.DMA((len(sizes),)),
        ]
    else:
        out_shape = jax.ShapeDtypeStruct((ROWS, 768), jnp.float32)
        out_specs = VMEM
    return pl.pallas_call(
        functools.partial(project_kernel, count, acc is not None, last, joint),
        in_specs=specs,
        out_specs=out_specs,
        out_shape=out_shape,
        scratch_shapes=scratch,
        compiler_params=pltpu.CompilerParams(vmem_limit_bytes=58 * 2**20),
        cost_estimate=pl.CostEstimate(flops=1, bytes_accessed=1, transcendentals=0),
        name="project",
    )(*operands)


def attend_kernel(info, old_map, *refs):
    packed, packed_other, late, late_source = refs[:4], refs[4], refs[5:13], refs[13:15]
    out, query, keys, values, top, total, accum, late_other, sems = refs[15:]
    copies = [pltpu.make_async_copy(late_source[i], late_other.at[i], sems.at[i]) for i in range(2)]
    for copy in copies:
        copy.start()
    me = info[0]
    high, z, core = me // 8, lax.rem(me // 2, 4), lax.rem(me, 2)
    for swapped in range(2):
        for r, (dh, dz) in enumerate(CHIPS):
            if swapped and r % 4 == 0:
                copies[r // 4].wait()
            source = lax.rem(high + dh, 2) * 8 + lax.rem(z + 4 - dz, 4) * 2 + lax.rem(core + swapped, 2)
            slot = info[3 + source]
            for j in range(CHUNKS):
                if j == 0:
                    ref, base = (packed_other, (dz * 2 + dh) * PAYLOAD) if swapped else (packed[dz], dh * PAYLOAD)
                else:
                    ref, base = (late_other.at[r // 4], (r % 4) * PAYLOAD) if swapped else (late[r], 0)
                for k in range(16):
                    at = pl.ds(pl.multiple_of(old_map[source * 16 + k] * FINE + j * W, W), W)
                    rows = slice(base + k * W, base + (k + 1) * W)
                    keys[at, :] = ref[rows, 0:HEAD]
                    values[at, :] = ref[rows, HEAD : 2 * HEAD]
                for h in range(4):
                    at = pl.ds(pl.multiple_of(base + ROWS + (core * 2 + h // 2) * W, W), W)
                    to = (slot // 8) * 1024 + h * 256 + lax.rem(slot, 8) * FINE + j * W
                    query[pl.ds(pl.multiple_of(to, W), W), :] = ref[at, (h % 2) * HEAD : (h % 2 + 1) * HEAD]

    for u in range(2):
        coarse = info[1 + u]
        queries = query[u * 1024 : (u + 1) * 1024, :]
        top[...] = jnp.full(top.shape, -1e30, jnp.float32)
        total[...] = jnp.zeros_like(total)
        accum[...] = jnp.zeros_like(accum)
        whole = (coarse * 256) // KB

        def absorb(block, masked, coarse=coarse, queries=queries):
            start = pl.multiple_of(block * KB, KB)
            scores = dot_t(queries, keys[pl.ds(start, KB), :])
            if masked:
                row = lax.rem(lax.broadcasted_iota(jnp.int32, (1024, KB), 0), 256) + coarse * 256
                visible = lax.broadcasted_iota(jnp.int32, (1024, KB), 1) + start <= row
                scores = jnp.where(visible, scores, -1e30)
            old = top[...]
            new = jnp.maximum(old, jnp.max(fold(scores, jnp.maximum), axis=-1, keepdims=True))
            factor = jnp.exp2((old - new) * (SCALE * LOG2E))
            weights = jnp.exp2(less(scores, new) * (SCALE * LOG2E))
            if masked:
                weights = jnp.where(visible, weights, 0.0)
            total[...] = total[...] * factor + fold(weights, jnp.add)
            accum[...] = accum[...] * factor + dot(
                weights.astype(jnp.bfloat16), values[pl.ds(start, KB), :]
            )
            top[...] = new

        def body(block, carry, absorb=absorb):
            absorb(block, False)
            return carry

        lax.fori_loop(0, whole, body, 0)
        absorb(whole, True)
        result = accum[...] / jnp.sum(total[...], axis=-1, keepdims=True)
        for h in range(4):
            out[u * 256 : (u + 1) * 256, h * HEAD : (h + 1) * HEAD] = result[h * 256 : (h + 1) * 256].astype(
                jnp.bfloat16
            )


def attend(info, old_map, parts):
    return pl.pallas_call(
        attend_kernel,
        out_shape=jax.ShapeDtypeStruct((512, 512), jnp.bfloat16),
        in_specs=[SMEM, SMEM] + [VMEM] * (len(parts) - 2) + [HBM] * 2,
        out_specs=VMEM,
        scratch_shapes=[
            pltpu.VMEM((2048, HEAD), jnp.bfloat16),
            pltpu.VMEM((8192, HEAD), jnp.bfloat16),
            pltpu.VMEM((8192, HEAD), jnp.bfloat16),
            pltpu.VMEM((1024, HEAD), jnp.float32),
            pltpu.VMEM((1024, HEAD), jnp.float32),
            pltpu.VMEM((1024, HEAD), jnp.float32),
            pltpu.VMEM((2, 4 * PAYLOAD, 256), jnp.bfloat16),
            pltpu.SemaphoreType.DMA((2,)),
        ],
        compiler_params=pltpu.CompilerParams(vmem_limit_bytes=56 * 2**20),
        name="attend",
    )(info, old_map, *parts)


def routing(old_map, new_map, own_index):
    devices = jnp.arange(16, dtype=jnp.int32)
    old_mine = lax.dynamic_index_in_dim(old_map, own_index, 0, keepdims=False)
    new_mine = lax.dynamic_index_in_dim(new_map, own_index, 0, keepdims=False)
    outward = jnp.any(new_map[:, :, None] == old_mine[None, None, :], axis=1)
    send_order = jnp.sum(outward.astype(jnp.int32) * devices[None, :], axis=1)
    inward = jnp.any(old_map[:, :, None] == new_mine[None, None, :], axis=1)
    slot_of = jnp.sum(inward.astype(jnp.int32) * devices[None, :], axis=1)
    coarse = jnp.stack([new_mine[0] // 8, new_mine[8] // 8])
    return (
        jnp.concatenate([own_index[None], send_order]).astype(jnp.int32),
        jnp.concatenate([own_index[None], coarse, slot_of]).astype(jnp.int32),
        old_mine,
    )


def angle_tables(positions):
    half = HEAD // 2
    freqs = jnp.exp(jnp.arange(half, dtype=jnp.float32) * (-2.0 * math.log(THETA) / HEAD))
    angles = positions.astype(jnp.float32)[:, None] * freqs[None, :]
    cosine = jnp.cos(angles)
    sine = jnp.sin(angles)
    return jnp.concatenate([cosine, cosine], axis=1), jnp.concatenate([-sine, sine], axis=1)


def local(tokens, old_map, new_map, w_query, key_projection_weight, value_projection_weight):
    me = lax.axis_index("ctx").astype(jnp.int32)
    place = lax.axis_index("tp").astype(jnp.int32)
    weights = (w_query, key_projection_weight, value_projection_weight)
    send_info, attend_info, old_mine = routing(old_map, new_map, me)
    x, y = place // 2, place % 2
    feature = lambda dx, dy: ((x + dx) % 4) * 2 + (y + dy) % 2
    order = [(0, 0), (3, 0), (1, 0), (0, 1), (3, 1), (2, 0), (1, 1), (2, 1)]
    features = jnp.stack([feature(dx, dy) for dx, dy in order]).astype(jnp.int32)
    chunks = tokens.reshape(16, CHUNKS, W, 1024)
    early, late = (chunks[:, j].reshape(ROWS, 1024) for j in range(CHUNKS))
    tables = []
    for j in range(CHUNKS):
        positions = old_mine[:, None] * FINE + j * W + jnp.arange(W, dtype=jnp.int32)[None, :]
        tables += angle_tables(positions.reshape(-1))
    old_flat = old_map.reshape(-1)

    left = shift_x(early, 1)
    right = shift_x(early, -1)
    across = swap_y(early)
    late, left, right, across, send_info, attend_info, old_flat, *tables = together(
        late, left, right, across, send_info, attend_info, old_flat, *tables
    )
    left_across = shift_x(across, 1)
    far = shift_x(right, -1)
    right_across = swap_y(right)
    late_across = swap_y(late)
    total = project(features[:4], [early, left, right, across], weights)
    left_across, far, late = together(left_across, far, after(late, total))
    late_right = shift_x(late, -1)
    far_across = shift_x(left_across, 1)
    right_across = after(right_across, late)
    total = project(features[4:7], [left_across, far, right_across], weights, total)
    late_right, total = together(late_right, total)
    late_far = shift_x(late_right, -1)
    late_right_across = swap_y(late_right)
    far_across = after(far_across, late_right)
    late_left = shift_x(after(late, far_across), 1)
    sent = project(features[7:], [far_across], weights, total, (send_info, *tables[:2]), joint=True)
    partner = shift_ctx(sent[4], 1, 0)
    late_across, late_left = together(late_across, late_left, sent[0])[:2]
    late_left_across = shift_x(late_across, 1)
    total = project(features[:4], [late, late_left, late_right, late_across], weights)
    late_far, late_right_across = together(late_far, late_right_across)
    late_far_across = shift_x(late_right_across, -1)
    partner, total = together(partner, total)
    early_parts = [
        jnp.concatenate([sent[dz], partner[:ROWS], partner[ROWS + dz * 4 * W : ROWS + (dz + 1) * 4 * W]], axis=0)
        for dz in range(4)
    ]
    *early_parts, total = together(*early_parts, total)
    total = project(features[5:7], [late_far, late_right_across], weights, total)
    early_parts[1:] = [shift_ctx(early_parts[dz], 0, dz) for dz in range(1, 4)]
    last = jnp.stack([features[4], features[7]])
    tail = [late_left_across, late_far_across]
    sent = project(last, tail, weights, total, (send_info, *tables[2:]))
    early_other = swap_core(jnp.concatenate(early_parts, axis=0))
    sent = list(sent)
    late_parts = [shift_ctx(sent[r], *CHIPS[r]) for r in range(4, 8)]
    early_parts[1], late_parts[0], *sent[:4] = together(early_parts[1], late_parts[0], *sent[:4])
    late_parts = [sent[0]] + [shift_ctx(sent[r], *CHIPS[r]) for r in range(1, 4)] + late_parts
    late_other = [swap_core(jnp.concatenate(late_parts[at : at + 4], axis=0)) for at in (0, 4)]
    return attend(attend_info, old_flat, [*early_parts, early_other, *late_parts, *late_other])


def solution(mesh):
    return jax.shard_map(
        local,
        mesh=mesh,
        in_specs=(P("ctx", "tp"), P(), P(), P(None, "tp"), P(None, "tp"), P(None, "tp")),
        out_specs=P("ctx", "tp"),
        check_vma=False,
    )
```

```python
import functools
import math

import jax
import jax.numpy as jnp
from jax import lax
from jax.experimental import pallas as pl
from jax.experimental.pallas import tpu as pltpu
from jax.sharding import PartitionSpec as P

HEAD = 128
THETA = 500000.0
SCALE = HEAD ** -0.5
LOG2E = math.log2(math.e)
FINE = 32
CHUNKS = 2
W = FINE // CHUNKS
ROWS = 16 * W
PAYLOAD = 20 * W
KB = 512
VMEM = pl.BlockSpec(memory_space=pltpu.VMEM)
SMEM = pl.BlockSpec(memory_space=pltpu.SMEM)

CHIPS = [(dh, dz) for dh in range(2) for dz in range(4)]


def shift_x(block, step):
    perm = [(i * 2 + j, ((i + step) % 4) * 2 + j) for i in range(4) for j in range(2)]
    return lax.ppermute(block, "tp", perm)


def swap_y(block):
    return lax.ppermute(block, "tp", [(i, i ^ 1) for i in range(8)])


def shift_ctx(block, dh, dz):
    perm = [
        (h * 8 + z * 2 + c, (h ^ dh) * 8 + ((z + dz) % 4) * 2 + c)
        for h in range(2)
        for z in range(4)
        for c in range(2)
    ]
    return lax.ppermute(block, "ctx", perm)


def together(*values):
    return lax.optimization_barrier(values)


def after(value, *others):
    return lax.optimization_barrier((value, *others))[0]


def swap_core(block):
    return lax.ppermute(block, "ctx", [(i, i ^ 1) for i in range(16)])


def dot(a, b):
    return lax.dot_general(a, b, (((1,), (0,)), ((), ())), preferred_element_type=jnp.float32)


def dot_t(a, b):
    return lax.dot_general(a, b, (((1,), (1,)), ((), ())), preferred_element_type=jnp.float32)


def fold(block, combine):
    result = block[:, :HEAD]
    for at in range(HEAD, block.shape[1], HEAD):
        result = combine(result, block[:, at : at + HEAD])
    return result


def less(block, lanes):
    return jnp.concatenate([block[:, at : at + HEAD] - lanes for at in range(0, block.shape[1], HEAD)], axis=1)


def project_kernel(groups, has_acc, last, joint, *refs):
    features, refs = refs[0], refs[1:]
    blocks, at = [], 0
    for n in groups:
        blocks.append(refs[at : at + n])
        at += n
    wq, wk, wv = refs[at : at + 3]
    at += 3
    acc_in = None
    if has_acc:
        acc_in = refs[at]
        at += 1
    if last:
        info, cosine, sine = refs[at : at + 3]
        at += 3
        outs = refs[at:-2]
        acc, heads = refs[-2:]
    else:
        out, acc = refs[at : at + 2]
    step = pl.program_id(0)

    for i, parts in enumerate(blocks):

        @pl.when(step == i)
        def add(i=i, parts=parts):
            block = parts[0][...] if len(parts) == 1 else jnp.concatenate([p[...] for p in parts], axis=0)
            for lo, hi, w in ((0, 512, wq[...]), (512, 768, jnp.concatenate([wk[...], wv[...]], axis=1))):
                value = dot(block, w)
                if i > 0:
                    value = value + acc[:, lo:hi]
                elif has_acc:
                    value = value + acc_in[:, lo:hi]
                acc[:, lo:hi] = value

    @pl.when(step == len(blocks) - 1)
    def finish():
        if not last:
            out[...] = acc[...]
            return
        cos, sin = cosine[...], sine[...]

        def rotated(lo):
            vector = acc[:, lo : lo + HEAD]
            return (vector * cos + pltpu.roll(vector, HEAD // 2, 1) * sin).astype(jnp.bfloat16)

        for h in range(4):
            heads[:, h * HEAD : (h + 1) * HEAD] = rotated(h * HEAD)
        key = rotated(512)
        value = acc[:, 640:768].astype(jnp.bfloat16)
        me = info[0]
        high, z = me // 8, lax.rem(me // 2, 4)
        for payload in outs:
            payload[0:ROWS, 0:HEAD] = key
            payload[0:ROWS, HEAD : 2 * HEAD] = value
        for r, (dh, dz) in enumerate(CHIPS):
            to, base = (outs[4], dz * 4 * W) if joint and dh else (outs[r], 0)
            chip = lax.rem(high + dh, 2) * 8 + lax.rem(z + dz, 4) * 2
            for core in range(2):
                k = info[1 + chip + core]
                rows = pl.ds(pl.multiple_of(k * W, W), W)
                for half in range(2):
                    at = ROWS + base + (core * 2 + half) * W
                    to[at : at + W, :] = heads[rows, half * 256 : half * 256 + 256]


def project(features, blocks, weights, acc=None, tables=None, joint=False):
    groups = [len(b) for b in blocks]
    flat = [p for b in blocks for p in b]
    whole = lambda shape: pl.BlockSpec(shape, lambda i, f: (0,) * len(shape))
    last = tables is not None
    specs = [whole(p.shape) for p in flat]
    specs += [pl.BlockSpec((1024, w.shape[1]), lambda i, f: (f[i], 0)) for w in weights]
    operands = flat + list(weights)
    if acc is not None:
        specs.append(whole(acc.shape))
        operands.append(acc)
    scratch = [pltpu.VMEM((ROWS, 768), jnp.float32)]
    if last:
        specs += [SMEM, whole((ROWS, HEAD)), whole((ROWS, HEAD))]
        operands += list(tables)
        sizes = [PAYLOAD] * 4 + [2 * ROWS] if joint else [PAYLOAD] * 8
        out_shape = [jax.ShapeDtypeStruct((n, 256), jnp.bfloat16) for n in sizes]
        out_specs = [whole((n, 256)) for n in sizes]
        scratch.append(pltpu.VMEM((ROWS, 512), jnp.bfloat16))
    else:
        out_shape = jax.ShapeDtypeStruct((ROWS, 768), jnp.float32)
        out_specs = whole((ROWS, 768))
    return pl.pallas_call(
        functools.partial(project_kernel, groups, acc is not None, last, joint),
        grid_spec=pltpu.PrefetchScalarGridSpec(
            num_scalar_prefetch=1,
            grid=(len(blocks),),
            in_specs=specs,
            out_specs=out_specs,
            scratch_shapes=scratch,
        ),
        out_shape=out_shape,
        compiler_params=pltpu.CompilerParams(vmem_limit_bytes=48 * 2**20),
        cost_estimate=pl.CostEstimate(flops=1, bytes_accessed=1, transcendentals=0),
        name="project",
    )(features, *operands)


def attend_kernel(info, old_map, *refs):
    packed, packed_other, late, late_other = refs[:4], refs[4], refs[5:13], refs[13:15]
    out, query, pairs, top, total, accum = refs[15:]
    me = info[0]
    high, z, core = me // 8, lax.rem(me // 2, 4), lax.rem(me, 2)
    for r, (dh, dz) in enumerate(CHIPS):
        for swapped in range(2):
            source = lax.rem(high + dh, 2) * 8 + lax.rem(z + 4 - dz, 4) * 2 + lax.rem(core + swapped, 2)
            slot = info[3 + source]
            for j in range(CHUNKS):
                if j == 0:
                    ref, base = (packed_other, (dz * 2 + dh) * PAYLOAD) if swapped else (packed[dz], dh * PAYLOAD)
                else:
                    ref, base = (late_other[r // 4], (r % 4) * PAYLOAD) if swapped else (late[r], 0)
                for k in range(16):
                    at = pl.ds(pl.multiple_of(old_map[source * 16 + k] * FINE + j * W, W), W)
                    rows = slice(base + k * W, base + (k + 1) * W)
                    pairs[at, :] = ref[rows, :]
                for h in range(4):
                    at = pl.ds(pl.multiple_of(base + ROWS + (core * 2 + h // 2) * W, W), W)
                    to = (slot // 8) * 1024 + h * 256 + lax.rem(slot, 8) * FINE + j * W
                    query[pl.ds(pl.multiple_of(to, W), W), :] = ref[at, (h % 2) * HEAD : (h % 2 + 1) * HEAD]

    for u in range(2):
        coarse = info[1 + u]
        queries = query[u * 1024 : (u + 1) * 1024, :]
        top[...] = jnp.full(top.shape, -1e30, jnp.float32)
        total[...] = jnp.zeros_like(total)
        accum[...] = jnp.zeros_like(accum)
        whole = (coarse * 256) // KB

        def absorb(block, masked, coarse=coarse, queries=queries):
            start = pl.multiple_of(block * KB, KB)
            scores = dot_t(queries, pairs[pl.ds(start, KB), 0:HEAD])
            if masked:
                row = lax.rem(lax.broadcasted_iota(jnp.int32, (1024, KB), 0), 256) + coarse * 256
                visible = lax.broadcasted_iota(jnp.int32, (1024, KB), 1) + start <= row
                scores = jnp.where(visible, scores, -1e30)
            old = top[...]
            new = jnp.maximum(old, jnp.max(fold(scores, jnp.maximum), axis=-1, keepdims=True))
            factor = jnp.exp2((old - new) * (SCALE * LOG2E))
            weights = jnp.exp2(less(scores, new) * (SCALE * LOG2E))
            if masked:
                weights = jnp.where(visible, weights, 0.0)
            total[...] = total[...] * factor + fold(weights, jnp.add)
            accum[...] = accum[...] * factor + dot(
                weights.astype(jnp.bfloat16), pairs[pl.ds(start, KB), HEAD : 2 * HEAD]
            )
            top[...] = new

        def body(block, carry, absorb=absorb):
            absorb(block, False)
            return carry

        lax.fori_loop(0, whole, body, 0)
        absorb(whole, True)
        result = accum[...] / jnp.sum(total[...], axis=-1, keepdims=True)
        for h in range(4):
            out[u * 256 : (u + 1) * 256, h * HEAD : (h + 1) * HEAD] = result[h * 256 : (h + 1) * 256].astype(
                jnp.bfloat16
            )


def attend(info, old_map, parts):
    return pl.pallas_call(
        attend_kernel,
        out_shape=jax.ShapeDtypeStruct((512, 512), jnp.bfloat16),
        in_specs=[SMEM, SMEM] + [VMEM] * len(parts),
        out_specs=VMEM,
        scratch_shapes=[
            pltpu.VMEM((2048, HEAD), jnp.bfloat16),
            pltpu.VMEM((8192, 2 * HEAD), jnp.bfloat16),
            pltpu.VMEM((1024, HEAD), jnp.float32),
            pltpu.VMEM((1024, HEAD), jnp.float32),
            pltpu.VMEM((1024, HEAD), jnp.float32),
        ],
        compiler_params=pltpu.CompilerParams(vmem_limit_bytes=56 * 2**20),
        name="attend",
    )(info, old_map, *parts)


def routing(old_map, new_map, own_index):
    devices = jnp.arange(16, dtype=jnp.int32)
    old_mine = lax.dynamic_index_in_dim(old_map, own_index, 0, keepdims=False)
    new_mine = lax.dynamic_index_in_dim(new_map, own_index, 0, keepdims=False)
    outward = jnp.any(new_map[:, :, None] == old_mine[None, None, :], axis=1)
    send_order = jnp.sum(outward.astype(jnp.int32) * devices[None, :], axis=1)
    inward = jnp.any(old_map[:, :, None] == new_mine[None, None, :], axis=1)
    slot_of = jnp.sum(inward.astype(jnp.int32) * devices[None, :], axis=1)
    coarse = jnp.stack([new_mine[0] // 8, new_mine[8] // 8])
    return (
        jnp.concatenate([own_index[None], send_order]).astype(jnp.int32),
        jnp.concatenate([own_index[None], coarse, slot_of]).astype(jnp.int32),
        old_mine,
    )


def angle_tables(positions):
    half = HEAD // 2
    freqs = jnp.exp(jnp.arange(half, dtype=jnp.float32) * (-2.0 * math.log(THETA) / HEAD))
    angles = positions.astype(jnp.float32)[:, None] * freqs[None, :]
    cosine = jnp.cos(angles)
    sine = jnp.sin(angles)
    return jnp.concatenate([cosine, cosine], axis=1), jnp.concatenate([-sine, sine], axis=1)


def local(tokens, old_map, new_map, w_query, key_projection_weight, value_projection_weight):
    me = lax.axis_index("ctx").astype(jnp.int32)
    place = lax.axis_index("tp").astype(jnp.int32)
    weights = (w_query, key_projection_weight, value_projection_weight)
    send_info, attend_info, old_mine = routing(old_map, new_map, me)
    x, y = place // 2, place % 2
    feature = lambda dx, dy: ((x + dx) % 4) * 2 + (y + dy) % 2
    order = [(0, 0), (3, 0), (1, 0), (0, 1), (3, 1), (2, 0), (1, 1), (2, 1)]
    features = jnp.stack([feature(dx, dy) for dx, dy in order]).astype(jnp.int32)
    chunks = tokens.reshape(16, CHUNKS, W, 1024)
    early, late = (chunks[:, j].reshape(ROWS, 1024) for j in range(CHUNKS))
    tables = []
    for j in range(CHUNKS):
        positions = old_mine[:, None] * FINE + j * W + jnp.arange(W, dtype=jnp.int32)[None, :]
        tables += angle_tables(positions.reshape(-1))
    old_flat = old_map.reshape(-1)

    left = shift_x(early, 1)
    right = shift_x(early, -1)
    across = swap_y(early)
    late, left, right, across, send_info, attend_info, old_flat, *tables = together(
        late, left, right, across, send_info, attend_info, old_flat, *tables
    )
    left_across = shift_x(across, 1)
    far = shift_x(right, -1)
    right_across = swap_y(right)
    late_across = swap_y(late)
    total = project(features[:4], [(early,), (left,), (right,), (across,)], weights)
    left_across, far, late = together(left_across, far, after(late, total))
    late_right = shift_x(late, -1)
    far_across = shift_x(left_across, 1)
    right_across = after(right_across, late)
    late_left = shift_x(after(late, right_across), 1)
    total = project(features[4:7], [(left_across,), (far,), (right_across,)], weights, total)
    late_right, late_across, total = together(late_right, late_across, total)
    late_far = shift_x(late_right, -1)
    late_right_across = swap_y(late_right)
    far_across = after(far_across, late_right)
    sent = project(features[7:], [(far_across,)], weights, total, (send_info, *tables[:2]), joint=True)
    partner = shift_ctx(sent[4], 1, 0)
    late_across, late_left = together(late_across, late_left, sent[0])[:2]
    late_left_across = shift_x(late_across, 1)
    blocks = [(late,), (late_right,), (late_across,)]
    total = project(jnp.stack([features[0], features[2], features[3]]), blocks, weights)
    late_far, late_right_across, total = together(late_far, late_right_across, total)
    late_far_across = shift_x(late_right_across, -1)
    early_parts = [
        jnp.concatenate([sent[dz], partner[:ROWS], partner[ROWS + dz * 4 * W : ROWS + (dz + 1) * 4 * W]], axis=0)
        for dz in range(4)
    ]
    *early_parts, total = together(*early_parts, total)
    blocks = [(late_left,), (late_far,), (late_right_across,)]
    total = project(jnp.stack([features[1], features[5], features[6]]), blocks, weights, total)
    early_parts[1:] = [shift_ctx(early_parts[dz], 0, dz) for dz in range(1, 4)]
    last = jnp.stack([features[4], features[7]])
    tail = [(late_left_across,), (late_far_across,)]
    sent = project(last, tail, weights, total, (send_info, *tables[2:]))
    early_other = swap_core(jnp.concatenate(early_parts, axis=0))
    sent = list(sent)
    late_parts = [shift_ctx(sent[r], *CHIPS[r]) for r in range(4, 8)]
    early_parts[1], late_parts[0], *sent[:4] = together(early_parts[1], late_parts[0], *sent[:4])
    late_parts = [sent[0]] + [shift_ctx(sent[r], *CHIPS[r]) for r in range(1, 4)] + late_parts
    late_other = [swap_core(jnp.concatenate(late_parts[at : at + 4], axis=0)) for at in (0, 4)]
    return attend(attend_info, old_flat, [*early_parts, early_other, *late_parts, *late_other])


def solution(mesh):
    return jax.shard_map(
        local,
        mesh=mesh,
        in_specs=(P("ctx", "tp"), P(), P(), P(None, "tp"), P(None, "tp"), P(None, "tp")),
        out_specs=P("ctx", "tp"),
        check_vma=False,
    )
```

```python
import functools
import math

import jax
import jax.numpy as jnp
from jax import lax
from jax.experimental import pallas as pl
from jax.experimental.pallas import tpu as pltpu
from jax.sharding import PartitionSpec as P

HEAD = 128
THETA = 500000.0
SCALE = HEAD ** -0.5
LOG2E = math.log2(math.e)
FINE = 32
CHUNKS = 2
W = FINE // CHUNKS
ROWS = 16 * W
PAYLOAD = 20 * W
KB = 512
VMEM = pl.BlockSpec(memory_space=pltpu.VMEM)
SMEM = pl.BlockSpec(memory_space=pltpu.SMEM)

CHIPS = [(dh, dz) for dh in range(2) for dz in range(4)]


def shift_x(block, step):
    perm = [(i * 2 + j, ((i + step) % 4) * 2 + j) for i in range(4) for j in range(2)]
    return lax.ppermute(block, "tp", perm)


def swap_y(block):
    return lax.ppermute(block, "tp", [(i, i ^ 1) for i in range(8)])


def shift_ctx(block, dh, dz):
    perm = [
        (h * 8 + z * 2 + c, (h ^ dh) * 8 + ((z + dz) % 4) * 2 + c)
        for h in range(2)
        for z in range(4)
        for c in range(2)
    ]
    return lax.ppermute(block, "ctx", perm)


def together(*values):
    return lax.optimization_barrier(values)


def after(value, *others):
    return lax.optimization_barrier((value, *others))[0]


def swap_core(block):
    return lax.ppermute(block, "ctx", [(i, i ^ 1) for i in range(16)])


def dot(a, b):
    return lax.dot_general(a, b, (((1,), (0,)), ((), ())), preferred_element_type=jnp.float32)


def dot_t(a, b):
    return lax.dot_general(a, b, (((1,), (1,)), ((), ())), preferred_element_type=jnp.float32)


def fold(block, combine):
    result = block[:, :HEAD]
    for at in range(HEAD, block.shape[1], HEAD):
        result = combine(result, block[:, at : at + HEAD])
    return result


def less(block, lanes):
    return jnp.concatenate([block[:, at : at + HEAD] - lanes for at in range(0, block.shape[1], HEAD)], axis=1)


def project_kernel(groups, has_acc, last, joint, *refs):
    features, refs = refs[0], refs[1:]
    blocks, at = [], 0
    for n in groups:
        blocks.append(refs[at : at + n])
        at += n
    wq, wk, wv = refs[at : at + 3]
    at += 3
    acc_in = None
    if has_acc:
        acc_in = refs[at]
        at += 1
    if last:
        info, cosine, sine = refs[at : at + 3]
        at += 3
        outs = refs[at:-2]
        acc, heads = refs[-2:]
    else:
        out, acc = refs[at : at + 2]
    step = pl.program_id(0)

    for i, parts in enumerate(blocks):

        @pl.when(step == i)
        def add(i=i, parts=parts):
            block = parts[0][...] if len(parts) == 1 else jnp.concatenate([p[...] for p in parts], axis=0)
            for lo, hi, w in ((0, 512, wq[...]), (512, 768, jnp.concatenate([wk[...], wv[...]], axis=1))):
                value = dot(block, w)
                if i > 0:
                    value = value + acc[:, lo:hi]
                elif has_acc:
                    value = value + acc_in[:, lo:hi]
                acc[:, lo:hi] = value

    @pl.when(step == len(blocks) - 1)
    def finish():
        if not last:
            out[...] = acc[...]
            return
        cos, sin = cosine[...], sine[...]

        def rotated(lo):
            vector = acc[:, lo : lo + HEAD]
            return (vector * cos + pltpu.roll(vector, HEAD // 2, 1) * sin).astype(jnp.bfloat16)

        for h in range(4):
            heads[:, h * HEAD : (h + 1) * HEAD] = rotated(h * HEAD)
        key = rotated(512)
        value = acc[:, 640:768].astype(jnp.bfloat16)
        me = info[0]
        high, z = me // 8, lax.rem(me // 2, 4)
        for payload in outs:
            payload[0:ROWS, 0:HEAD] = key
            payload[0:ROWS, HEAD : 2 * HEAD] = value
        for r, (dh, dz) in enumerate(CHIPS):
            to, base = (outs[4], dz * 4 * W) if joint and dh else (outs[r], 0)
            chip = lax.rem(high + dh, 2) * 8 + lax.rem(z + dz, 4) * 2
            for core in range(2):
                k = info[1 + chip + core]
                rows = pl.ds(pl.multiple_of(k * W, W), W)
                for half in range(2):
                    at = ROWS + base + (core * 2 + half) * W
                    to[at : at + W, :] = heads[rows, half * 256 : half * 256 + 256]


def project(features, blocks, weights, acc=None, tables=None, joint=False):
    groups = [len(b) for b in blocks]
    flat = [p for b in blocks for p in b]
    whole = lambda shape: pl.BlockSpec(shape, lambda i, f: (0,) * len(shape))
    last = tables is not None
    specs = [whole(p.shape) for p in flat]
    specs += [pl.BlockSpec((1024, w.shape[1]), lambda i, f: (f[i], 0)) for w in weights]
    operands = flat + list(weights)
    if acc is not None:
        specs.append(whole(acc.shape))
        operands.append(acc)
    scratch = [pltpu.VMEM((ROWS, 768), jnp.float32)]
    if last:
        specs += [SMEM, whole((ROWS, HEAD)), whole((ROWS, HEAD))]
        operands += list(tables)
        sizes = [PAYLOAD] * 4 + [2 * ROWS] if joint else [PAYLOAD] * 8
        out_shape = [jax.ShapeDtypeStruct((n, 256), jnp.bfloat16) for n in sizes]
        out_specs = [whole((n, 256)) for n in sizes]
        scratch.append(pltpu.VMEM((ROWS, 512), jnp.bfloat16))
    else:
        out_shape = jax.ShapeDtypeStruct((ROWS, 768), jnp.float32)
        out_specs = whole((ROWS, 768))
    return pl.pallas_call(
        functools.partial(project_kernel, groups, acc is not None, last, joint),
        grid_spec=pltpu.PrefetchScalarGridSpec(
            num_scalar_prefetch=1,
            grid=(len(blocks),),
            in_specs=specs,
            out_specs=out_specs,
            scratch_shapes=scratch,
        ),
        out_shape=out_shape,
        compiler_params=pltpu.CompilerParams(vmem_limit_bytes=48 * 2**20),
        cost_estimate=pl.CostEstimate(flops=1, bytes_accessed=1, transcendentals=0),
        name="project",
    )(features, *operands)


def attend_kernel(info, old_map, *refs):
    packed, packed_other, late, late_other = refs[:4], refs[4], refs[5:13], refs[13:15]
    out, query, pairs, top, total, accum = refs[15:]
    me = info[0]
    high, z, core = me // 8, lax.rem(me // 2, 4), lax.rem(me, 2)
    for r, (dh, dz) in enumerate(CHIPS):
        for swapped in range(2):
            source = lax.rem(high + dh, 2) * 8 + lax.rem(z + 4 - dz, 4) * 2 + lax.rem(core + swapped, 2)
            slot = info[3 + source]
            for j in range(CHUNKS):
                if j == 0:
                    ref, base = (packed_other, (dz * 2 + dh) * PAYLOAD) if swapped else (packed[dz], dh * PAYLOAD)
                else:
                    ref, base = (late_other[r // 4], (r % 4) * PAYLOAD) if swapped else (late[r], 0)
                for k in range(16):
                    at = pl.ds(pl.multiple_of(old_map[source * 16 + k] * FINE + j * W, W), W)
                    rows = slice(base + k * W, base + (k + 1) * W)
                    pairs[at, :] = ref[rows, :]
                for h in range(4):
                    at = pl.ds(pl.multiple_of(base + ROWS + (core * 2 + h // 2) * W, W), W)
                    to = (slot // 8) * 1024 + h * 256 + lax.rem(slot, 8) * FINE + j * W
                    query[pl.ds(pl.multiple_of(to, W), W), :] = ref[at, (h % 2) * HEAD : (h % 2 + 1) * HEAD]

    for u in range(2):
        coarse = info[1 + u]
        queries = query[u * 1024 : (u + 1) * 1024, :]
        top[...] = jnp.full(top.shape, -1e30, jnp.float32)
        total[...] = jnp.zeros_like(total)
        accum[...] = jnp.zeros_like(accum)
        whole = (coarse * 256) // KB

        def absorb(block, masked, coarse=coarse, queries=queries):
            start = pl.multiple_of(block * KB, KB)
            scores = dot_t(queries, pairs[pl.ds(start, KB), 0:HEAD])
            if masked:
                row = lax.rem(lax.broadcasted_iota(jnp.int32, (1024, KB), 0), 256) + coarse * 256
                visible = lax.broadcasted_iota(jnp.int32, (1024, KB), 1) + start <= row
                scores = jnp.where(visible, scores, -1e30)
            old = top[...]
            new = jnp.maximum(old, jnp.max(fold(scores, jnp.maximum), axis=-1, keepdims=True))
            factor = jnp.exp2((old - new) * (SCALE * LOG2E))
            weights = jnp.exp2(less(scores, new) * (SCALE * LOG2E))
            if masked:
                weights = jnp.where(visible, weights, 0.0)
            total[...] = total[...] * factor + fold(weights, jnp.add)
            accum[...] = accum[...] * factor + dot(
                weights.astype(jnp.bfloat16), pairs[pl.ds(start, KB), HEAD : 2 * HEAD]
            )
            top[...] = new

        def body(block, carry, absorb=absorb):
            absorb(block, False)
            return carry

        lax.fori_loop(0, whole, body, 0)
        absorb(whole, True)
        result = accum[...] / jnp.sum(total[...], axis=-1, keepdims=True)
        for h in range(4):
            out[u * 256 : (u + 1) * 256, h * HEAD : (h + 1) * HEAD] = result[h * 256 : (h + 1) * 256].astype(
                jnp.bfloat16
            )


def attend(info, old_map, parts):
    return pl.pallas_call(
        attend_kernel,
        out_shape=jax.ShapeDtypeStruct((512, 512), jnp.bfloat16),
        in_specs=[SMEM, SMEM] + [VMEM] * len(parts),
        out_specs=VMEM,
        scratch_shapes=[
            pltpu.VMEM((2048, HEAD), jnp.bfloat16),
            pltpu.VMEM((8192, 2 * HEAD), jnp.bfloat16),
            pltpu.VMEM((1024, HEAD), jnp.float32),
            pltpu.VMEM((1024, HEAD), jnp.float32),
            pltpu.VMEM((1024, HEAD), jnp.float32),
        ],
        compiler_params=pltpu.CompilerParams(vmem_limit_bytes=62 * 2**20),
        name="attend",
    )(info, old_map, *parts)


def routing(old_map, new_map, own_index):
    devices = jnp.arange(16, dtype=jnp.int32)
    old_mine = lax.dynamic_index_in_dim(old_map, own_index, 0, keepdims=False)
    new_mine = lax.dynamic_index_in_dim(new_map, own_index, 0, keepdims=False)
    outward = jnp.any(new_map[:, :, None] == old_mine[None, None, :], axis=1)
    send_order = jnp.sum(outward.astype(jnp.int32) * devices[None, :], axis=1)
    inward = jnp.any(old_map[:, :, None] == new_mine[None, None, :], axis=1)
    slot_of = jnp.sum(inward.astype(jnp.int32) * devices[None, :], axis=1)
    coarse = jnp.stack([new_mine[0] // 8, new_mine[8] // 8])
    return (
        jnp.concatenate([own_index[None], send_order]).astype(jnp.int32),
        jnp.concatenate([own_index[None], coarse, slot_of]).astype(jnp.int32),
        old_mine,
    )


def angle_tables(positions):
    half = HEAD // 2
    freqs = jnp.exp(jnp.arange(half, dtype=jnp.float32) * (-2.0 * math.log(THETA) / HEAD))
    angles = positions.astype(jnp.float32)[:, None] * freqs[None, :]
    cosine = jnp.cos(angles)
    sine = jnp.sin(angles)
    return jnp.concatenate([cosine, cosine], axis=1), jnp.concatenate([-sine, sine], axis=1)


def local(tokens, old_map, new_map, w_query, key_projection_weight, value_projection_weight):
    me = lax.axis_index("ctx").astype(jnp.int32)
    place = lax.axis_index("tp").astype(jnp.int32)
    weights = (w_query, key_projection_weight, value_projection_weight)
    send_info, attend_info, old_mine = routing(old_map, new_map, me)
    x, y = place // 2, place % 2
    feature = lambda dx, dy: ((x + dx) % 4) * 2 + (y + dy) % 2
    order = [(0, 0), (3, 0), (1, 0), (0, 1), (3, 1), (2, 0), (1, 1), (2, 1)]
    features = jnp.stack([feature(dx, dy) for dx, dy in order]).astype(jnp.int32)
    chunks = tokens.reshape(16, CHUNKS, W, 1024)
    early, late = (chunks[:, j].reshape(ROWS, 1024) for j in range(CHUNKS))
    tables = []
    for j in range(CHUNKS):
        positions = old_mine[:, None] * FINE + j * W + jnp.arange(W, dtype=jnp.int32)[None, :]
        tables += angle_tables(positions.reshape(-1))
    old_flat = old_map.reshape(-1)

    left = shift_x(early, 1)
    right = shift_x(early, -1)
    across = swap_y(early)
    late, left, right, across, send_info, attend_info, old_flat, *tables = together(
        late, left, right, across, send_info, attend_info, old_flat, *tables
    )
    left_across = shift_x(across, 1)
    far = shift_x(right, -1)
    right_across = swap_y(right)
    late_across = swap_y(late)
    total = project(features[:4], [(early,), (left,), (right,), (across,)], weights)
    left_across, far, late = together(left_across, far, after(late, total))
    late_right = shift_x(late, -1)
    far_across = shift_x(left_across, 1)
    right_across = after(right_across, late)
    late_left = shift_x(after(late, right_across), 1)
    total = project(features[4:7], [(left_across,), (far,), (right_across,)], weights, total)
    late_right, late_across, total = together(late_right, late_across, total)
    late_far = shift_x(late_right, -1)
    late_right_across = swap_y(late_right)
    far_across = after(far_across, late_right)
    sent = project(features[7:], [(far_across,)], weights, total, (send_info, *tables[:2]), joint=True)
    partner = shift_ctx(sent[4], 1, 0)
    late_across, late_left = together(late_across, late_left, sent[0])[:2]
    late_left_across = shift_x(late_across, 1)
    blocks = [(late,), (late_right,), (late_across,)]
    total = project(jnp.stack([features[0], features[2], features[3]]), blocks, weights)
    late_far, late_right_across, total = together(late_far, late_right_across, total)
    late_far_across = shift_x(late_right_across, -1)
    early_parts = [
        jnp.concatenate([sent[dz], partner[:ROWS], partner[ROWS + dz * 4 * W : ROWS + (dz + 1) * 4 * W]], axis=0)
        for dz in range(4)
    ]
    *early_parts, total = together(*early_parts, total)
    blocks = [(late_left,), (late_far,), (late_right_across,)]
    total = project(jnp.stack([features[1], features[5], features[6]]), blocks, weights, total)
    early_parts[1:] = [shift_ctx(early_parts[dz], 0, dz) for dz in range(1, 4)]
    last = jnp.stack([features[4], features[7]])
    tail = [(late_left_across,), (late_far_across,)]
    sent = project(last, tail, weights, total, (send_info, *tables[2:]))
    early_other = swap_core(jnp.concatenate(early_parts, axis=0))
    sent = list(sent)
    late_parts = [shift_ctx(sent[r], *CHIPS[r]) for r in range(4, 8)]
    early_parts[1], late_parts[0], *sent[:4] = together(early_parts[1], late_parts[0], *sent[:4])
    late_parts = [sent[0]] + [shift_ctx(sent[r], *CHIPS[r]) for r in range(1, 4)] + late_parts
    late_other = [swap_core(jnp.concatenate(late_parts[at : at + 4], axis=0)) for at in (0, 4)]
    return attend(attend_info, old_flat, [*early_parts, early_other, *late_parts, *late_other])


def solution(mesh):
    return jax.shard_map(
        local,
        mesh=mesh,
        in_specs=(P("ctx", "tp"), P(), P(), P(None, "tp"), P(None, "tp"), P(None, "tp")),
        out_specs=P("ctx", "tp"),
        check_vma=False,
    )
```

```python
import functools
import math

import jax
import jax.numpy as jnp
from jax import lax
from jax.experimental import pallas as pl
from jax.experimental.pallas import tpu as pltpu
from jax.sharding import PartitionSpec as P

HEAD = 128
THETA = 500000.0
SCALE = HEAD ** -0.5
LOG2E = math.log2(math.e)
FINE = 32
CHUNKS = 2
W = FINE // CHUNKS
ROWS = 16 * W
PAYLOAD = 20 * W
KB = 512
VMEM = pl.BlockSpec(memory_space=pltpu.VMEM)
SMEM = pl.BlockSpec(memory_space=pltpu.SMEM)

CHIPS = [(dh, dz) for dh in range(2) for dz in range(4)]


def shift_x(block, step):
    perm = [(i * 2 + j, ((i + step) % 4) * 2 + j) for i in range(4) for j in range(2)]
    return lax.ppermute(block, "tp", perm)


def swap_y(block):
    return lax.ppermute(block, "tp", [(i, i ^ 1) for i in range(8)])


def shift_ctx(block, dh, dz):
    perm = [
        (h * 8 + z * 2 + c, (h ^ dh) * 8 + ((z + dz) % 4) * 2 + c)
        for h in range(2)
        for z in range(4)
        for c in range(2)
    ]
    return lax.ppermute(block, "ctx", perm)


def together(*values):
    return lax.optimization_barrier(values)


def after(value, *others):
    return lax.optimization_barrier((value, *others))[0]


def swap_core(block):
    return lax.ppermute(block, "ctx", [(i, i ^ 1) for i in range(16)])


def dot(a, b):
    return lax.dot_general(a, b, (((1,), (0,)), ((), ())), preferred_element_type=jnp.float32)


def dot_t(a, b):
    return lax.dot_general(a, b, (((1,), (1,)), ((), ())), preferred_element_type=jnp.float32)


def fold(block, combine):
    result = block[:, :HEAD]
    for at in range(HEAD, block.shape[1], HEAD):
        result = combine(result, block[:, at : at + HEAD])
    return result


def less(block, lanes):
    return jnp.concatenate([block[:, at : at + HEAD] - lanes for at in range(0, block.shape[1], HEAD)], axis=1)


def project_kernel(groups, has_acc, last, joint, *refs):
    features, refs = refs[0], refs[1:]
    blocks, at = [], 0
    for n in groups:
        blocks.append(refs[at : at + n])
        at += n
    wq, wk, wv = refs[at : at + 3]
    at += 3
    acc_in = None
    if has_acc:
        acc_in = refs[at]
        at += 1
    if last:
        info, cosine, sine = refs[at : at + 3]
        at += 3
        outs = refs[at:-2]
        acc, heads = refs[-2:]
    else:
        out, acc = refs[at : at + 2]
    step = pl.program_id(0)

    for i, parts in enumerate(blocks):

        @pl.when(step == i)
        def add(i=i, parts=parts):
            block = parts[0][...] if len(parts) == 1 else jnp.concatenate([p[...] for p in parts], axis=0)
            for lo, hi, w in ((0, 512, wq[...]), (512, 768, jnp.concatenate([wk[...], wv[...]], axis=1))):
                value = dot(block, w)
                if i > 0:
                    value = value + acc[:, lo:hi]
                elif has_acc:
                    value = value + acc_in[:, lo:hi]
                acc[:, lo:hi] = value

    @pl.when(step == len(blocks) - 1)
    def finish():
        if not last:
            out[...] = acc[...]
            return
        cos, sin = cosine[...], sine[...]

        def rotated(lo):
            vector = acc[:, lo : lo + HEAD]
            return (vector * cos + pltpu.roll(vector, HEAD // 2, 1) * sin).astype(jnp.bfloat16)

        for h in range(4):
            heads[:, h * HEAD : (h + 1) * HEAD] = rotated(h * HEAD)
        key = rotated(512)
        value = acc[:, 640:768].astype(jnp.bfloat16)
        me = info[0]
        high, z = me // 8, lax.rem(me // 2, 4)
        for payload in outs:
            payload[0:ROWS, 0:HEAD] = key
            payload[0:ROWS, HEAD : 2 * HEAD] = value
        for r, (dh, dz) in enumerate(CHIPS):
            to, base = (outs[4], dz * 4 * W) if joint and dh else (outs[r], 0)
            chip = lax.rem(high + dh, 2) * 8 + lax.rem(z + dz, 4) * 2
            for core in range(2):
                k = info[1 + chip + core]
                rows = pl.ds(pl.multiple_of(k * W, W), W)
                for half in range(2):
                    at = ROWS + base + (core * 2 + half) * W
                    to[at : at + W, :] = heads[rows, half * 256 : half * 256 + 256]


def project(features, blocks, weights, acc=None, tables=None, joint=False):
    groups = [len(b) for b in blocks]
    flat = [p for b in blocks for p in b]
    whole = lambda shape: pl.BlockSpec(shape, lambda i, f: (0,) * len(shape))
    last = tables is not None
    specs = [whole(p.shape) for p in flat]
    specs += [pl.BlockSpec((1024, w.shape[1]), lambda i, f: (f[i], 0)) for w in weights]
    operands = flat + list(weights)
    if acc is not None:
        specs.append(whole(acc.shape))
        operands.append(acc)
    scratch = [pltpu.VMEM((ROWS, 768), jnp.float32)]
    if last:
        specs += [SMEM, whole((ROWS, HEAD)), whole((ROWS, HEAD))]
        operands += list(tables)
        sizes = [PAYLOAD] * 4 + [2 * ROWS] if joint else [PAYLOAD] * 8
        out_shape = [jax.ShapeDtypeStruct((n, 256), jnp.bfloat16) for n in sizes]
        out_specs = [whole((n, 256)) for n in sizes]
        scratch.append(pltpu.VMEM((ROWS, 512), jnp.bfloat16))
    else:
        out_shape = jax.ShapeDtypeStruct((ROWS, 768), jnp.float32)
        out_specs = whole((ROWS, 768))
    return pl.pallas_call(
        functools.partial(project_kernel, groups, acc is not None, last, joint),
        grid_spec=pltpu.PrefetchScalarGridSpec(
            num_scalar_prefetch=1,
            grid=(len(blocks),),
            in_specs=specs,
            out_specs=out_specs,
            scratch_shapes=scratch,
        ),
        out_shape=out_shape,
        compiler_params=pltpu.CompilerParams(vmem_limit_bytes=48 * 2**20),
        cost_estimate=pl.CostEstimate(flops=1, bytes_accessed=1, transcendentals=0),
        name="project",
    )(features, *operands)


def attend_kernel(info, old_map, *refs):
    packed, packed_other, late, late_other = refs[:4], refs[4], refs[5:13], refs[13:15]
    out, query, pairs, top, total, accum = refs[15:]
    me = info[0]
    high, z, core = me // 8, lax.rem(me // 2, 4), lax.rem(me, 2)
    for r, (dh, dz) in enumerate(CHIPS):
        for swapped in range(2):
            source = lax.rem(high + dh, 2) * 8 + lax.rem(z + 4 - dz, 4) * 2 + lax.rem(core + swapped, 2)
            slot = info[3 + source]
            for j in range(CHUNKS):
                if j == 0:
                    ref, base = (packed_other, (dz * 2 + dh) * PAYLOAD) if swapped else (packed[dz], dh * PAYLOAD)
                else:
                    if not swapped:
                        ref, base = late[r], 0
                    elif 1 <= r <= 3:
                        ref, base = late_other[0], (r - 1) * PAYLOAD
                    else:
                        ref, base = late_other[1], max(r - 3, 0) * PAYLOAD
                for k in range(16):
                    at = pl.ds(pl.multiple_of(old_map[source * 16 + k] * FINE + j * W, W), W)
                    rows = slice(base + k * W, base + (k + 1) * W)
                    pairs[at, :] = ref[rows, :]
                for h in range(4):
                    at = pl.ds(pl.multiple_of(base + ROWS + (core * 2 + h // 2) * W, W), W)
                    to = (slot // 8) * 1024 + h * 256 + lax.rem(slot, 8) * FINE + j * W
                    query[pl.ds(pl.multiple_of(to, W), W), :] = ref[at, (h % 2) * HEAD : (h % 2 + 1) * HEAD]

    for u in range(2):
        coarse = info[1 + u]
        queries = query[u * 1024 : (u + 1) * 1024, :]
        top[...] = jnp.full(top.shape, -1e30, jnp.float32)
        total[...] = jnp.zeros_like(total)
        accum[...] = jnp.zeros_like(accum)
        whole = (coarse * 256) // KB

        def absorb(block, masked, coarse=coarse, queries=queries):
            start = pl.multiple_of(block * KB, KB)
            scores = dot_t(queries, pairs[pl.ds(start, KB), 0:HEAD])
            if masked:
                row = lax.rem(lax.broadcasted_iota(jnp.int32, (1024, KB), 0), 256) + coarse * 256
                visible = lax.broadcasted_iota(jnp.int32, (1024, KB), 1) + start <= row
                scores = jnp.where(visible, scores, -1e30)
            old = top[...]
            new = jnp.maximum(old, jnp.max(fold(scores, jnp.maximum), axis=-1, keepdims=True))
            factor = jnp.exp2((old - new) * (SCALE * LOG2E))
            weights = jnp.exp2(less(scores, new) * (SCALE * LOG2E))
            if masked:
                weights = jnp.where(visible, weights, 0.0)
            total[...] = total[...] * factor + fold(weights, jnp.add)
            accum[...] = accum[...] * factor + dot(
                weights.astype(jnp.bfloat16), pairs[pl.ds(start, KB), HEAD : 2 * HEAD]
            )
            top[...] = new

        def body(block, carry, absorb=absorb):
            absorb(block, False)
            return carry

        lax.fori_loop(0, whole, body, 0)
        absorb(whole, True)
        result = accum[...] / jnp.sum(total[...], axis=-1, keepdims=True)
        for h in range(4):
            out[u * 256 : (u + 1) * 256, h * HEAD : (h + 1) * HEAD] = result[h * 256 : (h + 1) * 256].astype(
                jnp.bfloat16
            )


def attend(info, old_map, parts):
    return pl.pallas_call(
        attend_kernel,
        out_shape=jax.ShapeDtypeStruct((512, 512), jnp.bfloat16),
        in_specs=[SMEM, SMEM] + [VMEM] * len(parts),
        out_specs=VMEM,
        scratch_shapes=[
            pltpu.VMEM((2048, HEAD), jnp.bfloat16),
            pltpu.VMEM((8192, 2 * HEAD), jnp.bfloat16),
            pltpu.VMEM((1024, HEAD), jnp.float32),
            pltpu.VMEM((1024, HEAD), jnp.float32),
            pltpu.VMEM((1024, HEAD), jnp.float32),
        ],
        compiler_params=pltpu.CompilerParams(vmem_limit_bytes=62 * 2**20),
        name="attend",
    )(info, old_map, *parts)


def routing(old_map, new_map, own_index):
    devices = jnp.arange(16, dtype=jnp.int32)
    old_mine = lax.dynamic_index_in_dim(old_map, own_index, 0, keepdims=False)
    new_mine = lax.dynamic_index_in_dim(new_map, own_index, 0, keepdims=False)
    outward = jnp.any(new_map[:, :, None] == old_mine[None, None, :], axis=1)
    send_order = jnp.sum(outward.astype(jnp.int32) * devices[None, :], axis=1)
    inward = jnp.any(old_map[:, :, None] == new_mine[None, None, :], axis=1)
    slot_of = jnp.sum(inward.astype(jnp.int32) * devices[None, :], axis=1)
    coarse = jnp.stack([new_mine[0] // 8, new_mine[8] // 8])
    return (
        jnp.concatenate([own_index[None], send_order]).astype(jnp.int32),
        jnp.concatenate([own_index[None], coarse, slot_of]).astype(jnp.int32),
        old_mine,
    )


def angle_tables(positions):
    half = HEAD // 2
    freqs = jnp.exp(jnp.arange(half, dtype=jnp.float32) * (-2.0 * math.log(THETA) / HEAD))
    angles = positions.astype(jnp.float32)[:, None] * freqs[None, :]
    cosine = jnp.cos(angles)
    sine = jnp.sin(angles)
    return jnp.concatenate([cosine, cosine], axis=1), jnp.concatenate([-sine, sine], axis=1)


def local(tokens, old_map, new_map, w_query, key_projection_weight, value_projection_weight):
    me = lax.axis_index("ctx").astype(jnp.int32)
    place = lax.axis_index("tp").astype(jnp.int32)
    weights = (w_query, key_projection_weight, value_projection_weight)
    send_info, attend_info, old_mine = routing(old_map, new_map, me)
    x, y = place // 2, place % 2
    feature = lambda dx, dy: ((x + dx) % 4) * 2 + (y + dy) % 2
    order = [(0, 0), (3, 0), (1, 0), (0, 1), (3, 1), (2, 0), (1, 1), (2, 1)]
    features = jnp.stack([feature(dx, dy) for dx, dy in order]).astype(jnp.int32)
    chunks = tokens.reshape(16, CHUNKS, W, 1024)
    early, late = (chunks[:, j].reshape(ROWS, 1024) for j in range(CHUNKS))
    tables = []
    for j in range(CHUNKS):
        positions = old_mine[:, None] * FINE + j * W + jnp.arange(W, dtype=jnp.int32)[None, :]
        tables += angle_tables(positions.reshape(-1))
    old_flat = old_map.reshape(-1)

    left = shift_x(early, 1)
    right = shift_x(early, -1)
    across = swap_y(early)
    late, left, right, across, send_info, attend_info, old_flat, *tables = together(
        late, left, right, across, send_info, attend_info, old_flat, *tables
    )
    left_across = shift_x(across, 1)
    far = shift_x(right, -1)
    right_across = swap_y(right)
    late_across = swap_y(late)
    total = project(features[:4], [(early,), (left,), (right,), (across,)], weights)
    left_across, far, late = together(left_across, far, after(late, total))
    late_right = shift_x(late, -1)
    far_across = shift_x(left_across, 1)
    right_across = after(right_across, late)
    late_left = shift_x(after(late, right_across), 1)
    total = project(features[4:7], [(left_across,), (far,), (right_across,)], weights, total)
    late_right, late_across, total = together(late_right, late_across, total)
    late_far = shift_x(late_right, -1)
    late_right_across = swap_y(late_right)
    far_across = after(far_across, late_right)
    sent = project(features[7:], [(far_across,)], weights, total, (send_info, *tables[:2]), joint=True)
    partner = shift_ctx(sent[4], 1, 0)
    late_across, late_left = together(late_across, late_left, sent[0])[:2]
    late_left_across = shift_x(late_across, 1)
    blocks = [(late,), (late_right,), (late_across,)]
    total = project(jnp.stack([features[0], features[2], features[3]]), blocks, weights)
    late_far, late_right_across, total = together(late_far, late_right_across, total)
    late_far_across = shift_x(late_right_across, -1)
    early_parts = [
        jnp.concatenate([sent[dz], partner[:ROWS], partner[ROWS + dz * 4 * W : ROWS + (dz + 1) * 4 * W]], axis=0)
        for dz in range(4)
    ]
    *early_parts, total = together(*early_parts, total)
    blocks = [(late_left,), (late_far,), (late_right_across,)]
    total = project(jnp.stack([features[1], features[5], features[6]]), blocks, weights, total)
    early_parts[1:] = [shift_ctx(early_parts[dz], 0, dz) for dz in range(1, 4)]
    last = jnp.stack([features[4], features[7]])
    tail = [(late_left_across,), (late_far_across,)]
    sent = project(last, tail, weights, total, (send_info, *tables[2:]))
    early_other = swap_core(jnp.concatenate(early_parts, axis=0))
    sent = list(sent)
    late_parts = [shift_ctx(sent[r], *CHIPS[r]) for r in range(4, 8)]
    early_parts[1], late_parts[0], *sent[:4] = together(early_parts[1], late_parts[0], *sent[:4])
    late_parts = [sent[0]] + [shift_ctx(sent[r], *CHIPS[r]) for r in range(1, 4)] + late_parts
    groups = [late_parts[1:4], late_parts[:1] + late_parts[4:]]
    late_other = [swap_core(jnp.concatenate(group, axis=0)) for group in groups]
    return attend(attend_info, old_flat, [*early_parts, early_other, *late_parts, *late_other])


def solution(mesh):
    return jax.shard_map(
        local,
        mesh=mesh,
        in_specs=(P("ctx", "tp"), P(), P(), P(None, "tp"), P(None, "tp"), P(None, "tp")),
        out_specs=P("ctx", "tp"),
        check_vma=False,
    )
```
